128 devices in a mesh: cx: 8 (over y, core), cy: 16 (over z, x).
Axes of the slice: x: 4, y: 4, z: 4, core: 2. Of those that a mesh axis runs over, the one named last changes fastest.
Arguments:
- params: float32 [14, 2097152], P(None, ('cx', 'cy')), may hold values from -7 to 140, as said below
- requests: int32 [128, 128, 1], P(('cx', 'cy')), may hold values from 0 to 127, as said below
- lists: int32 [8192, 256], P(('cx', 'cy')), may hold values from 0 to 16383, as said below
- list_len: int32 [8192], P(('cx', 'cy')), may hold values from 64 to 256, as said below
- offsets: int32 [8192, 2], P(('cx', 'cy')), may hold values from 0 to 119, as said below
- cotangent: float32 [8192, 3, 256], P(('cx', 'cy')), may hold values from -6 to 6
Outputs:
- image: float32 [8192, 3, 256], P(('cx', 'cy'))
- grads: float32 [14, 2097152], P(None, ('cx', 'cy'))
The draws below stay inside these ranges and needn't reach their ends.
Inputs may be any that keep to these rules, and one draw needn't show every extreme that they name: `params`: row 2 (depth z) lies in [40, 80) and rises along every tile's list; rows 0 and 1 lie in [0, 16 * 120 z / 1100) and [0, 16 * 68 z / 1100); row 6 (quaternion w) lies in [1, 2]. `requests`: for every owner, each of its 128 blocks is requested exactly once over all devices and slots. The 64 lists of one device together hold each entry of its fetched buffer exactly once. `list_len`: some tile of every device has 256 live entries. `offsets`: column 0 lies below 120, column 1 below 68.
All inputs are finite; a program needn't handle non-finite values.
Results may differ from the reference program's by a relative error of at most 0.0003.
Values sent between devices are 32-bit elements; how exact they have to be, the bound alone decides.
A program may use at most 192 MiB of HBM per device.

```python
import math
import jax
import jax.numpy as jnp
from jax import lax

SIDE = 16
PIX = 256
FOCAL = 1100
VIEW_TX = 120
VIEW_TY = 68
BLOCK = 128
L = 256
TILES_DEV = 64
TILES = 8192
SLOTS = 1
BLK_DEV = 128
G_DEV = 16384
GAUSS = 2097152
FETCHED = 16384
N_CX = 8
N_CY = 16


def layout(key):
    ndev = TILES // TILES_DEV
    owner_keys = jax.random.split(jax.random.fold_in(key, 101), ndev)
    owner_perm = jax.vmap(lambda k: jax.random.permutation(k, BLK_DEV))(owner_keys).astype(jnp.int32)
    list_keys = jax.random.split(jax.random.fold_in(key, 102), ndev)
    list_perm = jax.vmap(lambda k: jax.random.permutation(k, FETCHED))(list_keys).astype(jnp.int32)
    tile_x = jax.random.randint(jax.random.fold_in(key, 103), (TILES,), 0, VIEW_TX, jnp.int32)
    tile_y = jax.random.randint(jax.random.fold_in(key, 104), (TILES,), 0, VIEW_TY, jnp.int32)
    tile_x = tile_x.at[0].set(VIEW_TX - 1)
    tile_y = tile_y.at[0].set(VIEW_TY - 1)
    return (owner_perm, list_perm, tile_x, tile_y)


def draw_params(key, part):
    owner_perm, list_perm, tile_x, tile_y = layout(key)
    key = jax.random.fold_in(key, 11)
    ndev = TILES // TILES_DEV
    device_rows = jnp.arange(ndev, dtype=jnp.int32)
    inv_owner = jnp.zeros((ndev, BLK_DEV), jnp.int32).at[device_rows[:, None], owner_perm].set(jnp.broadcast_to(jnp.arange(BLK_DEV, dtype=jnp.int32)[None, :], (ndev, BLK_DEV)))
    inv_list = jnp.zeros((ndev, FETCHED), jnp.int32).at[device_rows[:, None], list_perm].set(jnp.broadcast_to(jnp.arange(FETCHED, dtype=jnp.int32)[None, :], (ndev, FETCHED)))
    owner_of = device_rows[:, None, None]
    lane_of = jnp.arange(BLOCK, dtype=jnp.int32)[None, None, :]
    request_pos = inv_owner[:, :, None]
    asker = request_pos // SLOTS
    slot_of = request_pos % SLOTS
    place = (owner_of * SLOTS + slot_of) * BLOCK + lane_of
    asker_full = jnp.broadcast_to(asker, place.shape)
    list_pos = inv_list[asker_full, place].reshape(-1)
    home = asker_full.reshape(-1) * TILES_DEV + list_pos // L
    rank = (list_pos % L).astype(jnp.float32)
    home_x = jnp.take(tile_x, home).astype(jnp.float32)
    home_y = jnp.take(tile_y, home).astype(jnp.float32)
    key_u, key_n, key_e = jax.random.split(key, 3)
    unif = jax.random.uniform(key_u, (14, GAUSS), jnp.float32)
    norm = jnp.clip(jax.random.normal(key_n, (14, GAUSS), jnp.float32), -3.0, 3.0)
    extra = jax.random.uniform(key_e, (GAUSS,), jnp.float32)
    scale_lo, scale_hi, scale_pow = (math.log(0.05), math.log(0.2), 1.0)
    opac_lo, opac_hi, bright = (-6.0, -2.0, 0.0)
    depth = 40.0 + 40.0 * (rank + unif[2]) / L
    u_pix = SIDE * (home_x + unif[0])
    v_pix = SIDE * (home_y + unif[1])
    rows = [u_pix * depth / FOCAL, v_pix * depth / FOCAL, depth]
    rows = rows + [scale_lo + (scale_hi - scale_lo) * unif[3 + i] ** scale_pow for i in range(3)]
    rows = rows + [1.0 + unif[6], norm[7], norm[8], norm[9]]
    opacity = jnp.where(extra < bright, 4.6 + 2.4 * unif[10], opac_lo + (opac_hi - opac_lo) * unif[10])
    rows = rows + [opacity, unif[11], unif[12], unif[13]]
    return jnp.stack(rows)


def draw_requests(key, part):
    owner_perm, list_perm, tile_x, tile_y = layout(key)
    ndev = TILES // TILES_DEV
    return jnp.transpose(owner_perm.reshape(ndev, ndev, SLOTS), (1, 0, 2)).astype(jnp.int32)


def draw_lists(key, part):
    owner_perm, list_perm, tile_x, tile_y = layout(key)
    return list_perm.reshape(TILES, L).astype(jnp.int32)


def draw_offsets(key, part):
    owner_perm, list_perm, tile_x, tile_y = layout(key)
    return jnp.stack([tile_x, tile_y], axis=1).astype(jnp.int32)


def draw_list_len(key, part):
    key = jax.random.fold_in(key, 12)
    counts = jax.random.randint(key, (TILES,), L // 4, L + 1, jnp.int32)
    return counts.at[::TILES_DEV].set(L)


def block_scale(key, extent, cuts, smallest, largest):
    def one(axis_at, shards_of):
        draws = jax.random.uniform(jax.random.fold_in(jax.random.fold_in(key, 6), axis_at), (shards_of,), jnp.float32, smallest / len(cuts), largest / len(cuts))
        return jnp.repeat(jnp.exp(draws), extent[axis_at] // shards_of).reshape((-1,) + (1,) * (len(extent) - axis_at - 1))

    gain = one(*cuts[0])
    for cut in cuts[1:]:
        gain = gain * one(*cut)
    return gain


def centred(rng, shape, deviation, bound, shards=(), kind=jnp.bfloat16):
    loudness = block_scale(rng, shape, shards, -0.22, 0.18) if shards else 1.0
    values = jax.random.normal(rng, shape, jnp.float32) * deviation * loudness
    return jnp.minimum(jnp.maximum(values, -bound), bound).astype(kind)


def setup_inputs(seed: int = 0) -> dict:
    keys = jax.random.split(jax.random.key(seed), 7)
    params = draw_params(jax.random.fold_in(keys[6], 71), 0)
    requests = draw_requests(jax.random.fold_in(keys[6], 71), 0)
    lists = draw_lists(jax.random.fold_in(keys[6], 71), 0)
    list_len = draw_list_len(jax.random.fold_in(keys[6], 71), 0)
    offsets = draw_offsets(jax.random.fold_in(keys[6], 71), 0)
    cotangent = centred(keys[5], (TILES, 3, PIX), 1.0, 6.0, ((0, 128),), jnp.float32)
    return dict(params=params, requests=requests, lists=lists, list_len=list_len, offsets=offsets, cotangent=cotangent)


def project(params):
    focal = jnp.float32(FOCAL)
    xpos, ypos, depth = (params[0], params[1], params[2])
    svar = [jnp.exp(2.0 * params[3 + i]) for i in range(3)]
    qnorm = jnp.sqrt(params[6] ** 2 + params[7] ** 2 + params[8] ** 2 + params[9] ** 2)
    qw, qx, qy, qz = (params[6] / qnorm, params[7] / qnorm, params[8] / qnorm, params[9] / qnorm)
    rot = [[1.0 - 2.0 * (qy * qy + qz * qz), 2.0 * (qx * qy - qw * qz), 2.0 * (qx * qz + qw * qy)], [2.0 * (qx * qy + qw * qz), 1.0 - 2.0 * (qx * qx + qz * qz), 2.0 * (qy * qz - qw * qx)], [2.0 * (qx * qz - qw * qy), 2.0 * (qy * qz + qw * qx), 1.0 - 2.0 * (qx * qx + qy * qy)]]

    def sigma(i, j):
        return rot[i][0] * rot[j][0] * svar[0] + rot[i][1] * rot[j][1] * svar[1] + rot[i][2] * rot[j][2] * svar[2]
    j_diag = focal / depth
    j_xz = -focal * xpos / (depth * depth)
    j_yz = -focal * ypos / (depth * depth)
    cov_a = j_diag * j_diag * sigma(0, 0) + 2.0 * j_diag * j_xz * sigma(0, 2) + j_xz * j_xz * sigma(2, 2) + 0.3
    cov_b = j_diag * j_diag * sigma(0, 1) + j_diag * j_yz * sigma(0, 2) + j_xz * j_diag * sigma(1, 2) + j_xz * j_yz * sigma(2, 2)
    cov_c = j_diag * j_diag * sigma(1, 1) + 2.0 * j_diag * j_yz * sigma(1, 2) + j_yz * j_yz * sigma(2, 2) + 0.3
    determ = cov_a * cov_c - cov_b * cov_b
    return jnp.stack([focal * xpos / depth, focal * ypos / depth, cov_c / determ, -cov_b / determ, cov_a / determ, jax.nn.sigmoid(params[10]), params[11], params[12], params[13]])

def tile_image(features, live, offset):
    pixel = jnp.arange(PIX, dtype=jnp.int32)
    pos_x = (offset[0] * SIDE + pixel % SIDE).astype(jnp.float32) + 0.5
    pos_y = (offset[1] * SIDE + pixel // SIDE).astype(jnp.float32) + 0.5
    delta_x = pos_x[:, None] - features[0][None, :]
    delta_y = pos_y[:, None] - features[1][None, :]
    power = -0.5 * (features[2] * delta_x * delta_x + features[4] * delta_y * delta_y) - features[3] * delta_x * delta_y
    alpha = jnp.minimum(0.99, features[5] * jnp.exp(power)) * live[None, :]
    log_keep = jnp.log1p(-alpha)
    before = jnp.cumsum(log_keep, axis=1) - log_keep
    weight = alpha * jnp.exp(before)
    return jnp.dot(features[6:9], weight.T, precision=lax.Precision.HIGHEST)

def reference(params, requests, lists, list_len, offsets, cotangent):
    ndev = N_CX * N_CY
    feats = project(params)
    lanes = jnp.arange(BLOCK, dtype=jnp.int32)
    owners = jnp.arange(ndev, dtype=jnp.int32)
    entry = jnp.arange(L, dtype=jnp.int32)

    def one_device(carry, device):
        wanted = requests[device]
        gidx = ((owners[:, None] * G_DEV + wanted * BLOCK)[:, :, None] + lanes[None, None, :]).reshape(-1)
        fetched = jnp.take(feats, gidx, axis=1)
        start = (device * TILES_DEV).astype(jnp.int32)
        tile_lists = lax.dynamic_slice_in_dim(lists, start, TILES_DEV, 0)
        tile_lens = lax.dynamic_slice_in_dim(list_len, start, TILES_DEV, 0)
        tile_offsets = lax.dynamic_slice_in_dim(offsets, start, TILES_DEV, 0)
        tile_cots = lax.dynamic_slice_in_dim(cotangent, start, TILES_DEV, 0)

        def per_tile(entries, length, offset, cot):
            live = (entry < length).astype(jnp.float32)
            gathered = jnp.take(fetched, entries, axis=1)
            img, pull = jax.vjp(lambda f: tile_image(f, live, offset), gathered)
            return (img, pull(cot)[0])
        images, tgrads = jax.vmap(per_tile)(tile_lists, tile_lens, tile_offsets, tile_cots)
        where = jnp.take(gidx, tile_lists.reshape(-1))
        flat = jnp.moveaxis(tgrads, 1, 0).reshape(9, -1)
        return (carry.at[:, where].add(flat), images)
    gfeat, images = lax.scan(one_device, jnp.zeros((9, GAUSS), jnp.float32), owners)
    _, back = jax.vjp(project, params)
    return (images.reshape(TILES, 3, PIX), back(gfeat)[0])
```

```python
import functools

import jax
import jax.numpy as jnp
import numpy as np
from jax import lax
from jax.experimental import pallas as pl
from jax.experimental.pallas import tpu as pltpu
from jax.sharding import PartitionSpec as P

SIDE = 16
PIX = SIDE * SIDE
FOCAL = 1100.0
LANES = 128
TG = 8
NFEAT = 9
NPAR = 14
LOG2E = 1.4426950408889634
bf16 = jnp.bfloat16
f32 = jnp.float32
NT_DIMS = (((1,), (1,)), ((), ()))
AXES = ("cx", "cy")


def geometry(params):
    focal = jnp.float32(FOCAL)
    xpos, ypos, depth = params[0], params[1], params[2]
    svar = [jnp.exp(2.0 * params[3 + i]) for i in range(3)]
    qnorm = jnp.sqrt(params[6] ** 2 + params[7] ** 2 + params[8] ** 2 + params[9] ** 2)
    qw, qx, qy, qz = (params[6] / qnorm, params[7] / qnorm, params[8] / qnorm, params[9] / qnorm)
    rot = [
        [1.0 - 2.0 * (qy * qy + qz * qz), 2.0 * (qx * qy - qw * qz), 2.0 * (qx * qz + qw * qy)],
        [2.0 * (qx * qy + qw * qz), 1.0 - 2.0 * (qx * qx + qz * qz), 2.0 * (qy * qz - qw * qx)],
        [2.0 * (qx * qz - qw * qy), 2.0 * (qy * qz + qw * qx), 1.0 - 2.0 * (qx * qx + qy * qy)],
    ]

    def sigma(i, j):
        return (
            rot[i][0] * rot[j][0] * svar[0]
            + rot[i][1] * rot[j][1] * svar[1]
            + rot[i][2] * rot[j][2] * svar[2]
        )

    j_diag = focal / depth
    j_xz = -focal * xpos / (depth * depth)
    j_yz = -focal * ypos / (depth * depth)
    s02, s12, s22 = sigma(0, 2), sigma(1, 2), sigma(2, 2)
    cov_a = j_diag * j_diag * sigma(0, 0) + 2.0 * j_diag * j_xz * s02 + j_xz * j_xz * s22 + 0.3
    cov_b = (
        j_diag * j_diag * sigma(0, 1)
        + j_diag * j_yz * s02
        + j_xz * j_diag * s12
        + j_xz * j_yz * s22
    )
    cov_c = j_diag * j_diag * sigma(1, 1) + 2.0 * j_diag * j_yz * s12 + j_yz * j_yz * s22 + 0.3
    determ = cov_a * cov_c - cov_b * cov_b
    return (
        focal * xpos / depth,
        focal * ypos / depth,
        cov_c / determ,
        -cov_b / determ,
        cov_a / determ,
    )


def stage_blocks(params_ref, asked_ref, stage, blocks):
    @pl.loop(0, blocks, unroll=8)
    def _(r):
        col = pl.multiple_of(asked_ref[r] * LANES, LANES)
        stage[pl.ds(pl.multiple_of(r * 16, 16), NPAR), :] = params_ref[:, pl.ds(col, LANES)]


def project_kernel(params_ref, out_ref, stage):
    blocks = out_ref.shape[0]

    @pl.loop(0, blocks, unroll=8)
    def _(r):
        col = pl.multiple_of(r * LANES, LANES)
        stage[pl.ds(pl.multiple_of(r * 16, 16), NPAR), :] = params_ref[:, pl.ds(col, LANES)]

    @pl.loop(0, blocks // 8)
    def _(i):
        par = [stage[pl.ds(i * 128 + c, 8, stride=16), :] for c in range(NPAR)]
        feats = list(geometry(par))
        feats.append(-jnp.log(1.0 + jnp.exp(-par[10])))
        feats += par[11:14]
        for c in range(NFEAT):
            stage[pl.ds(i * 128 + c, 8, stride=16), :] = feats[c]

    @pl.loop(0, blocks, unroll=8)
    def _(r):
        out_ref[r] = stage[pl.ds(pl.multiple_of(r * 16, 16), NFEAT), :]


def place(device):
    minor = lax.axis_size("cy")
    return (device // minor, lax.rem(device, minor))


def position():
    return lax.axis_index("cx") * lax.axis_size("cy") + lax.axis_index("cy")


def greet(peers):
    me = position()
    barrier = pltpu.get_barrier_semaphore()

    @pl.loop(1, peers)
    def _(off):
        pl.semaphore_signal(
            barrier,
            inc=1,
            device_id=place(lax.rem(me + off, peers)),
            device_id_type=pl.DeviceIdType.MESH,
        )

    pl.semaphore_wait(barrier, peers - 1)


def exchange(source, target, send_sem, recv_sem, peers, fill=None):
    me = position()

    @pl.loop(1, peers)
    def _(off):
        peer = lax.rem(me + off, peers)
        if fill is not None:
            fill(peer)
        pltpu.make_async_remote_copy(
            src_ref=source.at[peer],
            dst_ref=target.at[me],
            send_sem=send_sem,
            recv_sem=recv_sem,
            device_id=place(peer),
            device_id_type=pl.DeviceIdType.MESH,
        ).start()

    if fill is not None:
        fill(me)
    target[me] = source[me]
    rest = pltpu.make_async_remote_copy(
        src_ref=source.at[pl.ds(0, peers - 1)],
        dst_ref=target.at[pl.ds(0, peers - 1)],
        send_sem=send_sem,
        recv_sem=recv_sem,
        device_id=place(lax.rem(me + 1, peers)),
        device_id_type=pl.DeviceIdType.MESH,
    )
    rest.wait_send()
    rest.wait_recv()


def fetch_kernel(
    req_ref, table_ref, out_ref, asked_ref, asked_v, asked_s, outgoing, send1, recv1, send2, recv2, local
):
    peers = table_ref.shape[0]
    greet(peers)
    exchange(req_ref, asked_v, send1, recv1, peers)
    copy = pltpu.make_async_copy(asked_v, asked_s, local)
    copy.start()
    copy.wait()
    asked_ref[...] = asked_v[...]

    def fill(peer):
        outgoing[peer] = table_ref[asked_s[peer, 0, 0]]

    exchange(outgoing, out_ref, send2, recv2, peers, fill)


def return_kernel(grad_ref, out_ref, send, recv):
    peers = grad_ref.shape[0]
    greet(peers)
    exchange(grad_ref, out_ref, send, recv, peers)


def unproject_kernel(params_ref, asked_ref, grad_ref, out_ref, stage):
    blocks = grad_ref.shape[0]
    stage_blocks(params_ref, asked_ref, stage, blocks)

    @pl.loop(0, blocks // 8)
    def _(i):
        par = [stage[pl.ds(i * 128 + c, 8, stride=16), :] for c in range(NPAR)]
        rows = pl.ds(pl.multiple_of(i * 8, 8), 8)
        grad = [grad_ref[rows, c, :] for c in range(NFEAT)]
        _, pull = jax.vjp(geometry, par[:10])
        res = list(pull(tuple(grad[:5]))[0])
        decay = jnp.exp(-par[10])
        res.append(grad[5] * (decay / (1.0 + decay)))
        res += grad[6:9]
        for c in range(NPAR):
            stage[pl.ds(i * 128 + c, 8, stride=16), :] = res[c]

    @pl.loop(0, blocks, unroll=8)
    def _(r):
        col = pl.multiple_of(asked_ref[r] * LANES, LANES)
        out_ref[:, pl.ds(col, LANES)] = stage[pl.ds(pl.multiple_of(r * 16, 16), NPAR), :]


def split(x, parts):
    out = []
    for _ in range(parts - 1):
        p = x.astype(bf16)
        out.append(p)
        x = x - p.astype(f32)
    out.append(x.astype(bf16))
    return out


def render_kernel(
    feat_ref, idx_ref, len_ref, ox_ref, oy_ref, cot_ref, mono_ref,
    img_ref, gf_ref,
    tab3, tab2, picked, lhs, qg, alpha, wmask, whi, wlo, dqhi, dqlo, colt, scat, rhs_sc, acc,
):
    groups, span = idx_ref.shape
    length = span // TG
    owners = feat_ref.shape[0]
    half = LANES // 2
    for c in range(NFEAT):
        xt = feat_ref[:, c, :].T
        rem = jnp.concatenate([xt[:half], xt[half:]], axis=1)
        for s, p in enumerate(split(rem, 3 if c < 2 else 2)):
            cols = slice(s * 2 * owners, (s + 1) * 2 * owners)
            if c < 2:
                tab3[c * half : (c + 1) * half, cols] = p
            else:
                tab2[(c - 2) * half : (c - 1) * half, cols] = p
    acc[...] = jnp.zeros_like(acc)
    part = 1024
    kio = lax.broadcasted_iota(jnp.int32, (2 * owners, part), 0)
    lio = lax.broadcasted_iota(jnp.int32, (half, part), 0)
    own = (lax.broadcasted_iota(jnp.int32, (TG, span), 0)) == (
        lax.broadcasted_iota(jnp.int32, (TG, span), 1) % TG
    )
    entry = lax.broadcasted_iota(jnp.int32, (1, span), 1) // TG
    mono = mono_ref[...]
    mono_b = mono.astype(bf16)

    @pl.loop(0, groups)
    def _(g):
        for t in range(span // part):
            idx = idx_ref[pl.ds(g, 1), t * part : (t + 1) * part]
            hi = ((idx >> 6) & 1) * owners + (idx >> 7)
            lo = idx & (half - 1)
            oh = jnp.where(kio == hi, 1.0, 0.0).astype(bf16)
            mine = lio == lo
            t3 = jnp.dot(
                tab3[...], jnp.concatenate([oh, oh, oh], axis=0), preferred_element_type=f32
            )
            t2 = jnp.dot(tab2[...], jnp.concatenate([oh, oh], axis=0), preferred_element_type=f32)
            for c in range(NFEAT):
                v = t3[c * half : (c + 1) * half] if c < 2 else t2[(c - 2) * half : (c - 1) * half]
                picked[c : c + 1, t * part : (t + 1) * part] = jnp.sum(
                    jnp.where(mine, v, 0.0), axis=0, keepdims=True
                )
        f = [picked[c : c + 1, :] for c in range(NFEAT)]
        live = entry < len_ref[pl.ds(g, 1), :]
        u = f[0] - ox_ref[pl.ds(g, 1), :]
        v = f[1] - oy_ref[pl.ds(g, 1), :]
        a, b, c2 = f[2], f[3], f[4]
        pu = a * u + b * v
        pv = c2 * v + b * u
        k0 = f[5] - 0.5 * (u * pu + v * pv)
        coef = [
            jnp.where(live, LOG2E * k0, -1e30),
            jnp.where(live, LOG2E * pu, 0.0),
            jnp.where(live, LOG2E * pv, 0.0),
            jnp.where(live, (-0.5 * LOG2E) * a, 0.0),
            jnp.where(live, -LOG2E * b, 0.0),
            jnp.where(live, (-0.5 * LOG2E) * c2, 0.0),
            jnp.zeros_like(u),
            jnp.zeros_like(u),
        ]
        coef = jnp.concatenate(coef, axis=0)
        rows = [p.astype(f32) for p in split(coef, 3)]
        rows.append(jnp.zeros((8, span), f32))
        col_hi, col_lo = [], []
        for c in range(3):
            h, l = split(f[6 + c], 2)
            col_hi.append(jnp.where(own, h.astype(f32), 0.0))
            col_lo.append(jnp.where(own, l.astype(f32), 0.0))
        rows += col_hi + col_hi + col_lo
        left = jnp.concatenate(rows + [jnp.zeros((24, span), f32)], axis=0)
        colt[...] = left[32:128].astype(bf16)
        for q in range(span // LANES):
            lhs[q * LANES : (q + 1) * LANES, :] = left[:, q * LANES : (q + 1) * LANES].T.astype(bf16)
        cot = jnp.concatenate(
            [
                jnp.concatenate(
                    [cot_ref[pl.ds(g * 6 * TG + 2 * c + h, TG, stride=6), :] for h in range(2)],
                    axis=1,
                )
                for c in range(3)
            ],
            axis=0,
        )
        cot_hi, cot_lo = split(cot, 2)
        right_q = jnp.concatenate([mono_b[:8]] * 3 + [jnp.zeros((8 + 96, PIX), bf16)], axis=0)
        right_g = jnp.concatenate(
            [jnp.zeros((32, PIX), bf16), cot_hi, cot_lo, cot_hi, jnp.zeros((24, PIX), bf16)], axis=0
        )
        qg[...] = jnp.dot(
            lhs[...], jnp.concatenate([right_q, right_g], axis=1), preferred_element_type=f32
        )

        def fwd(i, trans):
            base = pl.multiple_of(i * 128, 128)
            for s in range(8):
                ws = []
                for h in range(2):
                    at = pl.ds(base + s * 16 + h * 8, 8)
                    e = jnp.exp2(qg[at, :PIX])
                    al = jnp.minimum(e, 0.99)
                    w = al * trans
                    trans = trans - w
                    alpha[at, :] = al
                    wmask[at, :] = jnp.where(e < 0.99, w, 0.0)
                    ws.append(w)
                w2 = jnp.concatenate(ws, axis=0)
                w2h, w2l = split(w2, 2)
                at2 = pl.ds(base + s * 16, 16)
                whi[at2, :] = w2h
                wlo[at2, :] = w2l
            return trans

        lax.fori_loop(0, length // 16, fwd, jnp.ones((TG, PIX), f32))

        def bwd(n, behind):
            i = length // 16 - 1 - n
            base = pl.multiple_of(i * 128, 128)
            for s in reversed(range(8)):
                ds = [None, None]
                for h in (1, 0):
                    at = pl.ds(base + s * 16 + h * 8, 8)
                    d = qg[at, PIX:] - behind
                    behind = behind + alpha[at, :] * d
                    ds[h] = wmask[at, :] * d
                d2h, d2l = split(jnp.concatenate(ds, axis=0), 2)
                at2 = pl.ds(base + s * 16, 16)
                dqhi[at2, :] = d2h
                dqlo[at2, :] = d2l
            return behind

        lax.fori_loop(0, length // 16, bwd, jnp.zeros((TG, PIX), f32))

        ch, cl = colt[0:24, :], colt[48:72, :]
        img = jnp.dot(jnp.concatenate([ch, cl], axis=0), whi[...], preferred_element_type=f32)
        img = img[:24] + img[24:] + jnp.dot(ch, wlo[...], preferred_element_type=f32)
        for c in range(3):
            for h in range(2):
                img_ref[pl.ds(g * 6 * TG + 2 * c + h, TG, stride=6), :] = img[
                    c * TG : (c + 1) * TG, h * LANES : (h + 1) * LANES
                ]
        both = jnp.concatenate([cot_hi, cot_lo], axis=0)
        dcol = lax.dot_general(both, whi[...], NT_DIMS, preferred_element_type=f32)
        dcol = (
            dcol[:24] + dcol[24:]
            + lax.dot_general(cot_hi, wlo[...], NT_DIMS, preferred_element_type=f32)
        )
        mom = lax.dot_general(mono_b, dqhi[...], NT_DIMS, preferred_element_type=f32)
        mom = mom + lax.dot_general(mono_b, dqlo[...], NT_DIMS, preferred_element_type=f32)
        s0, sx, sy = mom[0:1], mom[1:2], mom[2:3]
        sxx, sxy, syy = mom[3:4], mom[4:5], mom[5:6]
        mx = sx - u * s0
        my = sy - v * s0
        mxx = sxx - u * (sx + mx)
        myy = syy - v * (sy + my)
        mxy = sxy - u * sy - v * mx
        out = [
            a * mx + b * my,
            c2 * my + b * mx,
            -0.5 * mxx,
            -mxy,
            -0.5 * myy,
            s0,
        ]
        for c in range(3):
            out.append(
                jnp.sum(jnp.where(own, dcol[c * TG : (c + 1) * TG], 0.0), axis=0, keepdims=True)
            )

        idx = idx_ref[pl.ds(g, 1), :]
        hio = lax.broadcasted_iota(jnp.int32, (owners // 2, span), 0)
        loo = lax.broadcasted_iota(jnp.int32, (2 * LANES, span), 0)
        hi = (idx >> 7) & (owners // 2 - 1)
        lo = ((idx >> 13) << 7) | (idx & (LANES - 1))
        oh = jnp.where(hio == hi, 1.0, 0.0).astype(bf16)
        ol = jnp.where(loo == lo, 1.0, 0.0).astype(bf16)
        rhs_sc[:, :span] = ol
        rhs_sc[:, span:] = ol
        hh = owners // 2
        for c in range(NFEAT):
            for s, p in enumerate(split(out[c], 2)):
                scat[c * hh : (c + 1) * hh, s * span : (s + 1) * span] = oh * p
        acc[...] += lax.dot_general(scat[...], rhs_sc[...], NT_DIMS, preferred_element_type=f32)

    hh = owners // 2
    for c in range(NFEAT):
        gf_ref[:hh, c, :] = acc[c * hh : (c + 1) * hh, :LANES]
        gf_ref[hh:, c, :] = acc[c * hh : (c + 1) * hh, LANES:]


def monomials():
    pix = np.arange(PIX)
    x = (pix % SIDE) - (SIDE - 1) / 2.0
    y = (pix // SIDE) - (SIDE - 1) / 2.0
    one = np.ones(PIX)
    return np.stack([one, x, y, x * x, x * y, y * y, 0 * one, 0 * one]).astype(np.float32)


VM = pl.BlockSpec(memory_space=pltpu.VMEM)
SM = pl.BlockSpec(memory_space=pltpu.SMEM)
LIMIT = pltpu.CompilerParams(vmem_limit_bytes=56 * 1024 * 1024)


def per_device(params, requests, lists, list_len, offsets, cotangent):
    peers = lax.axis_size(AXES)
    g_dev = params.shape[1]
    tiles, length = lists.shape
    groups = tiles // TG
    span = TG * length
    table = pl.pallas_call(
        project_kernel,
        out_shape=jax.ShapeDtypeStruct((peers, NFEAT, LANES), f32),
        in_specs=[VM],
        out_specs=VM,
        scratch_shapes=[pltpu.VMEM((peers * 16, LANES), f32)],
        compiler_params=LIMIT,
        name="project",
    )(params)
    wanted = jnp.broadcast_to(requests.reshape(peers, 1, 1), (peers, 1, LANES))
    fetched, asked = pl.pallas_call(
        fetch_kernel,
        out_shape=(
            jax.ShapeDtypeStruct((peers, NFEAT, LANES), f32),
            jax.ShapeDtypeStruct((peers, 1, LANES), jnp.int32),
        ),
        in_specs=[VM, VM],
        out_specs=(VM, VM),
        scratch_shapes=[
            pltpu.VMEM((peers, 1, LANES), jnp.int32),
            pltpu.SMEM((peers, 1, LANES), jnp.int32),
            pltpu.VMEM((peers, NFEAT, LANES), f32),
        ]
        + [pltpu.SemaphoreType.DMA] * 5,
        compiler_params=pltpu.CompilerParams(
            collective_id=0, has_side_effects=True, vmem_limit_bytes=32 * 1024 * 1024
        ),
        name="fetch",
    )(wanted, table)
    asked = asked[:, 0, 0]

    idx = lists.reshape(groups, TG, length).transpose(0, 2, 1).reshape(groups, span)
    lens = jnp.tile(list_len.reshape(groups, TG), (1, length))
    centre = (offsets * SIDE + SIDE // 2).astype(f32)
    ox = jnp.tile(centre[:, 0].reshape(groups, TG), (1, length))
    oy = jnp.tile(centre[:, 1].reshape(groups, TG), (1, length))
    image, gfeat = pl.pallas_call(
        render_kernel,
        out_shape=(
            jax.ShapeDtypeStruct((tiles * 6, LANES), f32),
            jax.ShapeDtypeStruct((peers, NFEAT, LANES), f32),
        ),
        in_specs=[VM] * 7,
        out_specs=(VM, VM),
        scratch_shapes=[
            pltpu.VMEM((LANES, 6 * peers), bf16),
            pltpu.VMEM((7 * LANES // 2, 4 * peers), bf16),
            pltpu.VMEM((16, span), f32),
            pltpu.VMEM((span, LANES), bf16),
            pltpu.VMEM((span, 2 * PIX), f32),
            pltpu.VMEM((span, PIX), f32),
            pltpu.VMEM((span, PIX), f32),
            pltpu.VMEM((span, PIX), bf16),
            pltpu.VMEM((span, PIX), bf16),
            pltpu.VMEM((span, PIX), bf16),
            pltpu.VMEM((span, PIX), bf16),
            pltpu.VMEM((96, span), bf16),
            pltpu.VMEM((NFEAT * peers // 2, 2 * span), bf16),
            pltpu.VMEM((2 * LANES, 2 * span), bf16),
            pltpu.VMEM((NFEAT * peers // 2, 2 * LANES), f32),
        ],
        compiler_params=LIMIT,
        name="render",
    )(fetched, idx, lens, ox, oy, cotangent.reshape(tiles * 6, LANES), jnp.asarray(monomials()))

    landed = pl.pallas_call(
        return_kernel,
        out_shape=jax.ShapeDtypeStruct((peers, NFEAT, LANES), f32),
        in_specs=[VM],
        out_specs=VM,
        scratch_shapes=[pltpu.SemaphoreType.DMA] * 2,
        compiler_params=pltpu.CompilerParams(
            collective_id=1, has_side_effects=True, vmem_limit_bytes=32 * 1024 * 1024
        ),
        name="give_back",
    )(gfeat)
    grads = pl.pallas_call(
        unproject_kernel,
        out_shape=jax.ShapeDtypeStruct((NPAR, g_dev), f32),
        in_specs=[VM, SM, VM],
        out_specs=VM,
        scratch_shapes=[pltpu.VMEM((peers * 16, LANES), f32)],
        compiler_params=LIMIT,
        name="unproject",
    )(params, asked, landed)
    return image.reshape(tiles, 3, PIX), grads


def solution(mesh):
    in_specs = (
        P(None, AXES),
        P(AXES, None, None),
        P(AXES, None),
        P(AXES),
        P(AXES, None),
        P(AXES, None, None),
    )
    out_specs = (P(AXES, None, None), P(None, AXES))
    return jax.shard_map(
        per_device, mesh=mesh, in_specs=in_specs, out_specs=out_specs, check_vma=False
    )
```

```python
import functools

import jax
import jax.numpy as jnp
import numpy as np
from jax import lax
from jax.experimental import pallas as pl
from jax.experimental.pallas import tpu as pltpu
from jax.sharding import PartitionSpec as P

SIDE = 16
PIX = SIDE * SIDE
FOCAL = 1100.0
LANES = 128
TG = 8
NFEAT = 9
NPAR = 14
LOG2E = 1.4426950408889634
NT_DIMS = (((1,), (1,)), ((), ()))
bf16 = jnp.bfloat16
f32 = jnp.float32
AXES = ("cx", "cy")


def geometry(params):
    focal = jnp.float32(FOCAL)
    xpos, ypos, depth = params[0], params[1], params[2]
    svar = [jnp.exp(2.0 * params[3 + i]) for i in range(3)]
    qnorm = jnp.sqrt(params[6] ** 2 + params[7] ** 2 + params[8] ** 2 + params[9] ** 2)
    qw, qx, qy, qz = (params[6] / qnorm, params[7] / qnorm, params[8] / qnorm, params[9] / qnorm)
    rot = [
        [1.0 - 2.0 * (qy * qy + qz * qz), 2.0 * (qx * qy - qw * qz), 2.0 * (qx * qz + qw * qy)],
        [2.0 * (qx * qy + qw * qz), 1.0 - 2.0 * (qx * qx + qz * qz), 2.0 * (qy * qz - qw * qx)],
        [2.0 * (qx * qz - qw * qy), 2.0 * (qy * qz + qw * qx), 1.0 - 2.0 * (qx * qx + qy * qy)],
    ]

    def sigma(i, j):
        return (
            rot[i][0] * rot[j][0] * svar[0]
            + rot[i][1] * rot[j][1] * svar[1]
            + rot[i][2] * rot[j][2] * svar[2]
        )

    j_diag = focal / depth
    j_xz = -focal * xpos / (depth * depth)
    j_yz = -focal * ypos / (depth * depth)
    s02, s12, s22 = sigma(0, 2), sigma(1, 2), sigma(2, 2)
    cov_a = j_diag * j_diag * sigma(0, 0) + 2.0 * j_diag * j_xz * s02 + j_xz * j_xz * s22 + 0.3
    cov_b = (
        j_diag * j_diag * sigma(0, 1)
        + j_diag * j_yz * s02
        + j_xz * j_diag * s12
        + j_xz * j_yz * s22
    )
    cov_c = j_diag * j_diag * sigma(1, 1) + 2.0 * j_diag * j_yz * s12 + j_yz * j_yz * s22 + 0.3
    determ = cov_a * cov_c - cov_b * cov_b
    return (
        focal * xpos / depth,
        focal * ypos / depth,
        cov_c / determ,
        -cov_b / determ,
        cov_a / determ,
    )


def stage_blocks(params_ref, asked_ref, stage, blocks):
    @pl.loop(0, blocks, unroll=8)
    def _(r):
        col = pl.multiple_of(asked_ref[r] * LANES, LANES)
        stage[pl.ds(pl.multiple_of(r * 16, 16), NPAR), :] = params_ref[:, pl.ds(col, LANES)]


def project(params_ref, out_ref, stage):
    blocks = out_ref.shape[0]

    @pl.loop(0, blocks, unroll=8)
    def _(r):
        col = pl.multiple_of(r * LANES, LANES)
        stage[pl.ds(pl.multiple_of(r * 16, 16), NPAR), :] = params_ref[:, pl.ds(col, LANES)]

    @pl.loop(0, blocks // 8)
    def _(i):
        par = [stage[pl.ds(i * 128 + c, 8, stride=16), :] for c in range(NPAR)]
        feats = list(geometry(par))
        feats.append(-jnp.log(1.0 + jnp.exp(-par[10])))
        feats += par[11:14]
        for c in range(NFEAT):
            stage[pl.ds(i * 128 + c, 8, stride=16), :] = feats[c]

    @pl.loop(0, blocks, unroll=8)
    def _(r):
        out_ref[r] = stage[pl.ds(pl.multiple_of(r * 16, 16), NFEAT), :]


def place(device):
    minor = lax.axis_size("cy")
    return (device // minor, lax.rem(device, minor))


def position():
    return lax.axis_index("cx") * lax.axis_size("cy") + lax.axis_index("cy")


def greet(peers):
    me = position()
    barrier = pltpu.get_barrier_semaphore()

    @pl.loop(1, peers)
    def _(off):
        pl.semaphore_signal(
            barrier,
            inc=1,
            device_id=place(lax.rem(me + off, peers)),
            device_id_type=pl.DeviceIdType.MESH,
        )

    pl.semaphore_wait(barrier, peers - 1)


def send(source, target, send_sem, recv_sem, peer):
    return pltpu.make_async_remote_copy(
        src_ref=source,
        dst_ref=target,
        send_sem=send_sem,
        recv_sem=recv_sem,
        device_id=place(peer),
        device_id_type=pl.DeviceIdType.MESH,
    )


def await_all(source, target, send_sem, recv_sem, peers):
    rest = send(
        source.at[pl.ds(0, peers - 1)],
        target.at[pl.ds(0, peers - 1)],
        send_sem,
        recv_sem,
        lax.rem(position() + 1, peers),
    )
    rest.wait_send()
    rest.wait_recv()


def invert(idx_ref, inv_ref, acc):
    steps, part = idx_ref.shape
    owners = inv_ref.shape[0]
    half = owners // 2
    hio = lax.broadcasted_iota(jnp.int32, (half, part), 0)
    loo = lax.broadcasted_iota(jnp.int32, (2 * LANES, part), 0)
    spot = lax.broadcasted_iota(jnp.int32, (1, part), 1)
    acc[...] = jnp.zeros_like(acc)

    @pl.loop(0, steps)
    def _(i):
        idx = idx_ref[pl.ds(i, 1), :]
        row = idx // LANES
        mine = hio == row % half
        high = (i * (part // LANES) + spot // LANES).astype(f32)
        low = (spot % LANES).astype(f32)
        left = jnp.concatenate(
            [jnp.where(mine, high, 0.0).astype(bf16), jnp.where(mine, low, 0.0).astype(bf16)], axis=0
        )
        lo = row // half * LANES + idx % LANES
        right = jnp.where(loo == lo, 1.0, 0.0).astype(bf16)
        acc[...] += lax.dot_general(left, right, NT_DIMS, preferred_element_type=f32)

    inv = acc[:half].astype(jnp.int32) * LANES + acc[half:].astype(jnp.int32)
    inv_ref[:half, :] = inv[:, :LANES]
    inv_ref[half:, :] = inv[:, LANES:]


def fetch_kernel(
    req_ref, params_ref, idx_ref,
    out_ref, asked_ref, inv_ref,
    asked_v, asked_s, table, stage, outgoing, acc, send1, recv1, send2, recv2, local,
):
    peers = out_ref.shape[0]
    me = position()
    greet(peers)

    @pl.loop(1, peers)
    def _(off):
        peer = lax.rem(me + off, peers)
        send(req_ref.at[peer], asked_v.at[me], send1, recv1, peer).start()

    asked_v[me] = req_ref[me]
    project(params_ref, table, stage)
    await_all(req_ref, asked_v, send1, recv1, peers)
    copy = pltpu.make_async_copy(asked_v, asked_s, local)
    copy.start()
    copy.wait()

    @pl.loop(1, peers)
    def _(off):
        peer = lax.rem(me + off, peers)
        outgoing[peer] = table[asked_s[peer, 0, 0]]
        send(outgoing.at[peer], out_ref.at[me], send2, recv2, peer).start()

    out_ref[me] = table[asked_s[me, 0, 0]]

    @pl.loop(0, peers)
    def _(d):
        asked_ref[d] = asked_s[d, 0, 0]

    invert(idx_ref, inv_ref, acc)
    await_all(outgoing, out_ref, send2, recv2, peers)


def return_kernel(
    grad_ref, inv_ref, out_ref, tabg, folded, outgoing, send_sem, recv_sem
):
    peers = out_ref.shape[0]
    me = position()
    steps = peers // 8
    greet(peers)
    fill_table(lambda c: grad_ref[c * LANES : (c + 1) * LANES, :], None, tabg, 0)

    @pl.loop(0, steps)
    def _(n):
        t = lax.rem(me // 8 + n, steps)
        idx = jnp.concatenate([inv_ref[pl.ds(t * 8 + q, 1), :] for q in range(8)], axis=1)
        rows = pick(idx, None, tabg, 0, folded)
        for c in range(NFEAT):
            outgoing[pl.ds(t * 8, 8), c, :] = rows[c]

        @pl.loop(0, 8)
        def _(q):
            peer = t * 8 + q

            @pl.when(peer != me)
            def _():
                send(outgoing.at[peer], out_ref.at[me], send_sem, recv_sem, peer).start()

    out_ref[me] = outgoing[me]
    await_all(outgoing, out_ref, send_sem, recv_sem, peers)


def unproject_kernel(params_ref, asked_ref, grad_ref, out_ref, stage):
    blocks = grad_ref.shape[0]
    stage_blocks(params_ref, asked_ref, stage, blocks)

    @pl.loop(0, blocks // 8)
    def _(i):
        par = [stage[pl.ds(i * 128 + c, 8, stride=16), :] for c in range(NPAR)]
        rows = pl.ds(pl.multiple_of(i * 8, 8), 8)
        grad = [grad_ref[rows, c, :] for c in range(NFEAT)]
        _, pull = jax.vjp(geometry, par[:10])
        res = list(pull(tuple(grad[:5]))[0])
        decay = jnp.exp(-par[10])
        res.append(grad[5] * (decay / (1.0 + decay)))
        res += grad[6:9]
        for c in range(NPAR):
            stage[pl.ds(i * 128 + c, 8, stride=16), :] = res[c]

    @pl.loop(0, blocks, unroll=8)
    def _(r):
        col = pl.multiple_of(asked_ref[r] * LANES, LANES)
        out_ref[:, pl.ds(col, LANES)] = stage[pl.ds(pl.multiple_of(r * 16, 16), NPAR), :]


def split(x, parts):
    out = []
    for _ in range(parts - 1):
        p = x.astype(bf16)
        out.append(p)
        x = x - p.astype(f32)
    out.append(x.astype(bf16))
    return out


def fill_table(read, table3, table2, deep):
    half = LANES // 2
    for c in range(NFEAT):
        xt = read(c).T
        n = 2 * xt.shape[1]
        rem = jnp.concatenate([xt[:half], xt[half:]], axis=1)
        for s, p in enumerate(split(rem, 3 if c < deep else 2)):
            if c < deep:
                table3[c * half : (c + 1) * half, s * n : (s + 1) * n] = p
            else:
                table2[(c - deep) * half : (c - deep + 1) * half, s * n : (s + 1) * n] = p


def pick(idx, table3, table2, deep, folded):
    half = LANES // 2
    n = idx.shape[1]
    rows = table2.shape[1] // 4
    kio = lax.broadcasted_iota(jnp.int32, (2 * rows, n), 0)
    lio = lax.broadcasted_iota(jnp.int32, (half, n), 0)
    hi = ((idx >> 6) & 1) * rows + (idx >> 7)
    mine = lio == (idx & (half - 1))
    oh = jnp.where(kio == hi, 1.0, 0.0).astype(bf16)
    if deep:
        t3 = jnp.dot(
            table3[...], jnp.concatenate([oh, oh, oh], axis=0), preferred_element_type=f32
        )
    t2 = jnp.dot(table2[...], jnp.concatenate([oh, oh], axis=0), preferred_element_type=f32)
    for c in range(NFEAT):
        if c < deep:
            v = t3[c * half : (c + 1) * half]
        else:
            v = t2[(c - deep) * half : (c - deep + 1) * half]
        v = jnp.where(mine, v, 0.0)
        part = v[0:8]
        for r in range(8, half, 8):
            part = part + v[r : r + 8]
        for q in range(n // LANES):
            folded[c * 64 + q * 8 : c * 64 + q * 8 + 8, :] = part[:, q * LANES : (q + 1) * LANES]
    out = []
    for c in range(NFEAT):
        total = folded[pl.ds(c * 64, 8, stride=8), :]
        for r in range(1, 8):
            total = total + folded[pl.ds(c * 64 + r, 8, stride=8), :]
        out.append(total)
    return out


PART = 1024
KC = 16
NB = 6
YS = [n + 0.5 for n in range(SIDE // 2)]


def swap_blocks(rows, lane):
    blk = lane // SIDE
    out = []
    for g in range(8):
        res = None
        for y in range(8):
            shift = ((y - g) * SIDE) % LANES
            r = pltpu.roll(rows[y], shift, 1) if shift else rows[y]
            res = r if res is None else jnp.where(blk == y, r, res)
        out.append(res)
    return out


def render_kernel(
    feat_ref, idx_ref, len_ref, off_ref, cot_ref, spread_ref, reduce_ref,
    img_ref, gsc_ref,
    tab3, tab2, folded, picked, stack, left, bcast, alpha, weight, trans, image, cots, moms, meta,
):
    steps = idx_ref.shape[0]
    fill_table(lambda c: feat_ref[:, c, :], tab3, tab2, 2)
    lane = lax.broadcasted_iota(jnp.int32, (8, LANES), 1)
    slot = lane % TG

    def per_tile(read):
        rows = []
        for g in range(8):
            row = jnp.full((1, LANES), read(g * TG), jnp.int32)
            for t in range(1, TG):
                row = jnp.where(slot[:1] == t, read(g * TG + t), row)
            rows.append(row)
        return jnp.concatenate(rows, axis=0)

    meta[0:8, :] = per_tile(lambda t: len_ref[t])
    meta[8:16, :] = per_tile(lambda t: off_ref[t, 0]) * SIDE + SIDE // 2
    meta[16:24, :] = per_tile(lambda t: off_ref[t, 1]) * SIDE + SIDE // 2
    stack[...] = jnp.zeros_like(stack)
    trans[...] = jnp.ones_like(trans)
    image[...] = jnp.zeros_like(image)
    for c in range(3):
        for h in range(2):
            rows = [cot_ref[pl.ds(g * 6 * TG + 2 * c + h, TG, stride=6), :] for g in range(8)]
            for y, val in enumerate(swap_blocks(rows, lane)):
                cots[(c * SIDE + h * 8 + y) * 8 : (c * SIDE + h * 8 + y + 1) * 8, :] = val

    def at_step(c, i):
        return pl.ds(pl.multiple_of(c * LANES + i * 8, 8), 8)

    @pl.loop(0, steps)
    def _(i):
        for c, val in enumerate(pick(idx_ref[pl.ds(i, 1), :], tab3, tab2, 2, folded)):
            picked[at_step(c, i), :] = val

    @pl.loop(0, steps)
    def _(i):
        f = [picked[at_step(c, i), :] for c in range(NFEAT)]
        live = (i * KC + lane // TG) < meta[0:8, :]
        u = f[0] - meta[8:16, :].astype(f32)
        v = f[1] - meta[16:24, :].astype(f32)
        a, b, c2 = f[2], f[3], f[4]
        picked[at_step(0, i), :] = u
        picked[at_step(1, i), :] = v
        pu = a * u + b * v
        pv = c2 * v + b * u
        k0 = f[5] - 0.5 * (u * pu + v * pv)
        vals = [
            jnp.where(live, LOG2E * k0, -1e30),
            jnp.where(live, LOG2E * pu, 0.0),
            jnp.where(live, LOG2E * pv, 0.0),
            jnp.where(live, (-0.5 * LOG2E) * a, 0.0),
            jnp.where(live, -LOG2E * b, 0.0),
            jnp.where(live, (-0.5 * LOG2E) * c2, 0.0),
            f[6],
            f[7],
            f[8],
        ]
        for n, val in enumerate(vals):
            for s, p in enumerate(split(val, 3)):
                at = s * 8 + n if n < 8 else 24 + s
                stack[pl.ds(at, 8, stride=32), :] = p.astype(f32)
        left[pl.ds(pl.multiple_of(i * LANES, LANES), LANES), :] = jnp.concatenate(
            [stack[:LANES].T, stack[LANES:].T], axis=1
        ).astype(bf16)

    bcast[...] = jnp.dot(left[...], spread_ref[...], preferred_element_type=f32)

    def forward(i):
        for hb in range(2):
            ys = list(range(4 * hb, 4 * hb + 4))
            spots = [(n, sg) for n in ys for sg in (1, -1)]
            yi = {(n, sg): (8 + n if sg > 0 else 7 - n) for n, sg in spots}
            tr = {p: trans[yi[p] * 8 : yi[p] * 8 + 8, :] for p in spots}
            im = {
                (c, p): image[(c * SIDE + yi[p]) * 8 : (c * SIDE + yi[p]) * 8 + 8, :]
                for p in spots
                for c in range(3)
            }
            for kl in range(KC):
                row = pl.ds(pl.multiple_of(i * (KC * 8) + kl * 8, 8), 8)
                pp, qq, rr, cr, cg, cb = [
                    bcast[row, n * LANES : (n + 1) * LANES] for n in range(NB)
                ]
                for n in ys:
                    even = pp + (YS[n] * YS[n]) * rr
                    odd = YS[n] * qq
                    for sg in (1, -1):
                        p = (n, sg)
                        e = jnp.exp2(even + odd if sg > 0 else even - odd)
                        al = jnp.minimum(e, 0.99)
                        w = al * tr[p]
                        tr[p] = tr[p] - w
                        at = pl.ds(pl.multiple_of((i * KC + kl) * PIX // 2 + yi[p] * 8, 8), 8)
                        alpha[at, :] = al
                        weight[at, :] = w
                        for c, col in enumerate((cr, cg, cb)):
                            im[c, p] = im[c, p] + col * w
            for p in spots:
                trans[yi[p] * 8 : yi[p] * 8 + 8, :] = tr[p]
                for c in range(3):
                    image[(c * SIDE + yi[p]) * 8 : (c * SIDE + yi[p]) * 8 + 8, :] = im[c, p]

    def backward(i):
        behind = {y: trans[y * 8 : y * 8 + 8, :] for y in range(SIDE)}
        for kl in reversed(range(KC)):
            row = pl.ds(pl.multiple_of(i * (KC * 8) + kl * 8, 8), 8)
            cols = [bcast[row, n * LANES : (n + 1) * LANES] for n in range(3, NB)]
            acc = [None] * NB

            def add(n, val):
                acc[n] = val if acc[n] is None else acc[n] + val

            for n in range(SIDE // 2):
                dq = {}
                for sg in (1, -1):
                    y = 8 + n if sg > 0 else 7 - n
                    at = pl.ds(pl.multiple_of((i * KC + kl) * PIX // 2 + y * 8, 8), 8)
                    al, w = alpha[at, :], weight[at, :]
                    ct = [cots[(c * SIDE + y) * 8 : (c * SIDE + y + 1) * 8, :] for c in range(3)]
                    d = cols[0] * ct[0] + cols[1] * ct[1] + cols[2] * ct[2] - behind[y]
                    behind[y] = behind[y] + al * d
                    dq[sg] = jnp.where(al < 0.99, w * d, 0.0)
                    for c in range(3):
                        add(3 + c, w * ct[c])
                both, diff = dq[1] + dq[-1], dq[1] - dq[-1]
                add(0, both)
                add(1, YS[n] * diff)
                add(2, (YS[n] * YS[n]) * both)
            for n in range(NB):
                bcast[row, n * LANES : (n + 1) * LANES] = acc[n]
        for y in range(SIDE):
            trans[y * 8 : y * 8 + 8, :] = behind[y]

    @pl.loop(0, steps)
    def _(i):
        forward(i)

    for c in range(3):
        for h in range(2):
            rows = [
                image[(c * SIDE + h * 8 + y) * 8 : (c * SIDE + h * 8 + y + 1) * 8, :]
                for y in range(8)
            ]
            for g, val in enumerate(swap_blocks(rows, lane)):
                img_ref[pl.ds(g * 6 * TG + 2 * c + h, TG, stride=6), :] = val

    trans[...] = jnp.zeros_like(trans)

    @pl.loop(0, steps)
    def _(n):
        backward(steps - 1 - n)

    batch = 4
    right = jnp.concatenate([reduce_ref[...]] * 3, axis=0)

    @pl.loop(0, steps // batch)
    def _(k):
        rows = pl.ds(pl.multiple_of(k * batch * LANES, LANES), batch * LANES)
        res = jnp.dot(
            jnp.concatenate(split(bcast[rows, :], 3), axis=1), right, preferred_element_type=f32
        )
        for q in range(batch):
            i = k * batch + q
            moms[q * LANES : (q + 1) * LANES, :] = res[q * LANES : (q + 1) * LANES].T
            m = [moms[pl.ds(q * LANES + n, 8, stride=16), :] for n in range(NFEAT)]
            u, v, a, b, c2 = [picked[at_step(n, i), :] for n in range(5)]
            s0, sx, sy, sxx, sxy, syy = m[:6]
            mx = sx - u * s0
            my = sy - v * s0
            out = [
                a * mx + b * my,
                c2 * my + b * mx,
                -0.5 * (sxx - u * (sx + mx)),
                -(sxy - u * sy - v * mx),
                -0.5 * (syy - v * (sy + my)),
                s0,
            ] + m[6:]
            for c in range(NFEAT):
                gsc_ref[at_step(c, i), :] = out[c]


def constants():
    x = np.arange(SIDE) - (SIDE - 1) / 2.0
    one = np.ones(SIDE)
    spread = np.zeros((8, 32, NB, 8, SIDE), np.float32)
    reduce = np.zeros((NB, 8, SIDE, 8, 16), np.float32)
    for g in range(8):
        for s in range(3):
            for row, q, val in (
                (0, 0, one), (1, 0, x), (3, 0, x * x), (2, 1, one), (4, 1, x), (5, 2, one),
                (6, 3, one), (7, 4, one),
            ):
                spread[g, s * 8 + row, q, g] = val
            spread[g, 24 + s, 5, g] = one
        for q, m, val in (
            (0, 0, one), (0, 1, x), (0, 3, x * x), (1, 2, one), (1, 4, x), (2, 5, one),
            (3, 6, one), (4, 7, one), (5, 8, one),
        ):
            reduce[q, g, :, g, m] = val
    return (
        jnp.asarray(spread.reshape(256, NB * LANES), bf16),
        jnp.asarray(reduce.reshape(NB * LANES, LANES), bf16),
    )


VM = pl.BlockSpec(memory_space=pltpu.VMEM)
SM = pl.BlockSpec(memory_space=pltpu.SMEM)
LIMIT = pltpu.CompilerParams(vmem_limit_bytes=56 * 1024 * 1024)


REMOTE = dict(has_side_effects=True, vmem_limit_bytes=40 * 1024 * 1024)


def fetch(requests, params, idx):
    peers = requests.shape[1]
    wanted = jnp.broadcast_to(requests.reshape(peers, 1, 1), (peers, 1, LANES))
    return pl.pallas_call(
        fetch_kernel,
        out_shape=(
            jax.ShapeDtypeStruct((peers, NFEAT, LANES), f32),
            jax.ShapeDtypeStruct((peers,), jnp.int32),
            jax.ShapeDtypeStruct((peers, LANES), jnp.int32),
        ),
        in_specs=[VM, VM, VM],
        out_specs=(VM, SM, VM),
        scratch_shapes=[
            pltpu.VMEM((peers, 1, LANES), jnp.int32),
            pltpu.SMEM((peers, 1, LANES), jnp.int32),
            pltpu.VMEM((peers, NFEAT, LANES), f32),
            pltpu.VMEM((peers * 16, LANES), f32),
            pltpu.VMEM((peers, NFEAT, LANES), f32),
            pltpu.VMEM((peers, 2 * LANES), f32),
        ]
        + [pltpu.SemaphoreType.DMA] * 5,
        compiler_params=pltpu.CompilerParams(collective_id=0, **REMOTE),
        name="fetch",
    )(wanted, params, idx)


def give_back(grads, inv):
    peers = inv.shape[0]
    return pl.pallas_call(
        return_kernel,
        out_shape=jax.ShapeDtypeStruct((peers, NFEAT, LANES), f32),
        in_specs=[VM, VM],
        out_specs=VM,
        scratch_shapes=[
            pltpu.VMEM((NFEAT * LANES // 2, 4 * LANES), bf16),
            pltpu.VMEM((NFEAT * 64, LANES), f32),
            pltpu.VMEM((peers, NFEAT, LANES), f32),
        ]
        + [pltpu.SemaphoreType.DMA] * 2,
        compiler_params=pltpu.CompilerParams(collective_id=1, **REMOTE),
        name="give_back",
    )(grads, inv)


def per_device(params, requests, lists, list_len, offsets, cotangent):
    peers = lax.axis_size(AXES)
    g_dev = params.shape[1]
    tiles, length = lists.shape
    steps = length // KC
    idx = lists.reshape(8, TG, steps, KC).transpose(2, 0, 3, 1).reshape(steps, PART)
    fetched, asked, inv = fetch(requests, params, idx)
    spread, reduce = constants()
    image, gfeat = pl.pallas_call(
        render_kernel,
        out_shape=(
            jax.ShapeDtypeStruct((tiles * 6, LANES), f32),
            jax.ShapeDtypeStruct((NFEAT * LANES, LANES), f32),
        ),
        in_specs=[VM, VM, SM, SM, VM, VM, VM],
        out_specs=(VM, VM),
        scratch_shapes=[
            pltpu.VMEM((LANES, 6 * peers), bf16),
            pltpu.VMEM((7 * LANES // 2, 4 * peers), bf16),
            pltpu.VMEM((NFEAT * 64, LANES), f32),
            pltpu.VMEM((NFEAT * LANES, LANES), f32),
            pltpu.VMEM((256, LANES), f32),
            pltpu.VMEM((length * 8, 256), bf16),
            pltpu.VMEM((length * 8, NB * LANES), f32),
            pltpu.VMEM((length * SIDE * 8, LANES), f32),
            pltpu.VMEM((length * SIDE * 8, LANES), f32),
            pltpu.VMEM((SIDE * 8, LANES), f32),
            pltpu.VMEM((3 * SIDE * 8, LANES), f32),
            pltpu.VMEM((3 * SIDE * 8, LANES), f32),
            pltpu.VMEM((4 * LANES, LANES), f32),
            pltpu.VMEM((24, LANES), jnp.int32),
        ],
        compiler_params=LIMIT,
        name="render",
    )(
        fetched,
        idx,
        list_len,
        offsets,
        cotangent.reshape(tiles * 6, LANES),
        spread,
        reduce,
    )

    landed = give_back(gfeat, inv)
    grads = pl.pallas_call(
        unproject_kernel,
        out_shape=jax.ShapeDtypeStruct((NPAR, g_dev), f32),
        in_specs=[VM, SM, VM],
        out_specs=VM,
        scratch_shapes=[pltpu.VMEM((peers * 16, LANES), f32)],
        compiler_params=LIMIT,
        name="unproject",
    )(params, asked, landed)
    return image.reshape(tiles, 3, PIX), grads


def solution(mesh):
    in_specs = (
        P(None, AXES),
        P(AXES, None, None),
        P(AXES, None),
        P(AXES),
        P(AXES, None),
        P(AXES, None, None),
    )
    out_specs = (P(AXES, None, None), P(None, AXES))
    return jax.shard_map(
        per_device, mesh=mesh, in_specs=in_specs, out_specs=out_specs, check_vma=False
    )
```

```python
import functools

import jax
import jax.numpy as jnp
import numpy as np
from jax import lax
from jax.experimental import pallas as pl
from jax.experimental.pallas import tpu as pltpu
from jax.sharding import PartitionSpec as P

SIDE = 16
PIX = SIDE * SIDE
FOCAL = 1100.0
LANES = 128
TG = 8
NFEAT = 9
NPAR = 14
LOG2E = 1.4426950408889634
NT_DIMS = (((1,), (1,)), ((), ()))
bf16 = jnp.bfloat16
f32 = jnp.float32
AXES = ("cx", "cy")


def geometry(params):
    focal = jnp.float32(FOCAL)
    xpos, ypos, depth = params[0], params[1], params[2]
    svar = [jnp.exp(2.0 * params[3 + i]) for i in range(3)]
    qnorm = jnp.sqrt(params[6] ** 2 + params[7] ** 2 + params[8] ** 2 + params[9] ** 2)
    qw, qx, qy, qz = (params[6] / qnorm, params[7] / qnorm, params[8] / qnorm, params[9] / qnorm)
    rot = [
        [1.0 - 2.0 * (qy * qy + qz * qz), 2.0 * (qx * qy - qw * qz), 2.0 * (qx * qz + qw * qy)],
        [2.0 * (qx * qy + qw * qz), 1.0 - 2.0 * (qx * qx + qz * qz), 2.0 * (qy * qz - qw * qx)],
        [2.0 * (qx * qz - qw * qy), 2.0 * (qy * qz + qw * qx), 1.0 - 2.0 * (qx * qx + qy * qy)],
    ]

    def sigma(i, j):
        return (
            rot[i][0] * rot[j][0] * svar[0]
            + rot[i][1] * rot[j][1] * svar[1]
            + rot[i][2] * rot[j][2] * svar[2]
        )

    j_diag = focal / depth
    j_xz = -focal * xpos / (depth * depth)
    j_yz = -focal * ypos / (depth * depth)
    s02, s12, s22 = sigma(0, 2), sigma(1, 2), sigma(2, 2)
    cov_a = j_diag * j_diag * sigma(0, 0) + 2.0 * j_diag * j_xz * s02 + j_xz * j_xz * s22 + 0.3
    cov_b = (
        j_diag * j_diag * sigma(0, 1)
        + j_diag * j_yz * s02
        + j_xz * j_diag * s12
        + j_xz * j_yz * s22
    )
    cov_c = j_diag * j_diag * sigma(1, 1) + 2.0 * j_diag * j_yz * s12 + j_yz * j_yz * s22 + 0.3
    determ = cov_a * cov_c - cov_b * cov_b
    return (
        focal * xpos / depth,
        focal * ypos / depth,
        cov_c / determ,
        -cov_b / determ,
        cov_a / determ,
    )


def stage_blocks(params_ref, asked_ref, stage, blocks):
    @pl.loop(0, blocks, unroll=8)
    def _(r):
        col = pl.multiple_of(asked_ref[r] * LANES, LANES)
        stage[pl.ds(pl.multiple_of(r * 16, 16), NPAR), :] = params_ref[:, pl.ds(col, LANES)]


def project(params_ref, out_ref, stage):
    blocks = out_ref.shape[0]

    @pl.loop(0, blocks, unroll=8)
    def _(r):
        col = pl.multiple_of(r * LANES, LANES)
        stage[pl.ds(pl.multiple_of(r * 16, 16), NPAR), :] = params_ref[:, pl.ds(col, LANES)]

    @pl.loop(0, blocks // 8)
    def _(i):
        par = [stage[pl.ds(i * 128 + c, 8, stride=16), :] for c in range(NPAR)]
        feats = list(geometry(par))
        feats.append(-jnp.log(1.0 + jnp.exp(-par[10])))
        feats += par[11:14]
        for c in range(NFEAT):
            stage[pl.ds(i * 128 + c, 8, stride=16), :] = feats[c]

    @pl.loop(0, blocks, unroll=8)
    def _(r):
        out_ref[r] = stage[pl.ds(pl.multiple_of(r * 16, 16), NFEAT), :]


def place(device):
    minor = lax.axis_size("cy")
    return (device // minor, lax.rem(device, minor))


def position():
    return lax.axis_index("cx") * lax.axis_size("cy") + lax.axis_index("cy")


def greet(peers):
    me = position()
    barrier = pltpu.get_barrier_semaphore()

    @pl.loop(1, peers)
    def _(off):
        pl.semaphore_signal(
            barrier,
            inc=1,
            device_id=place(lax.rem(me + off, peers)),
            device_id_type=pl.DeviceIdType.MESH,
        )


def hear(peers):
    pl.semaphore_wait(pltpu.get_barrier_semaphore(), peers - 1)


def send(source, target, send_sem, recv_sem, peer):
    return pltpu.make_async_remote_copy(
        src_ref=source,
        dst_ref=target,
        send_sem=send_sem,
        recv_sem=recv_sem,
        device_id=place(peer),
        device_id_type=pl.DeviceIdType.MESH,
    )


def await_all(source, target, send_sem, recv_sem, peers):
    rest = send(
        source.at[pl.ds(0, peers - 1)],
        target.at[pl.ds(0, peers - 1)],
        send_sem,
        recv_sem,
        lax.rem(position() + 1, peers),
    )
    rest.wait_send()
    rest.wait_recv()


def invert(idx_ref, inv_ref, acc):
    steps, part = idx_ref.shape[0] // 8, PART
    owners = inv_ref.shape[0]
    half = owners // 2
    hio = lax.broadcasted_iota(jnp.int32, (half, part), 0)
    loo = lax.broadcasted_iota(jnp.int32, (2 * LANES, part), 0)
    spot = lax.broadcasted_iota(jnp.int32, (1, part), 1)
    acc[...] = jnp.zeros_like(acc)

    @pl.loop(0, steps)
    def _(i):
        idx8 = idx_ref[rows8(i), :]
        idx = jnp.concatenate([idx8[q : q + 1] for q in range(8)], axis=1)
        row = idx // LANES
        mine = hio == row % half
        high = (i * (part // LANES) + spot // LANES).astype(f32)
        low = (spot % LANES).astype(f32)
        left = jnp.concatenate(
            [jnp.where(mine, high, 0.0).astype(bf16), jnp.where(mine, low, 0.0).astype(bf16)], axis=0
        )
        lo = row // half * LANES + idx % LANES
        right = jnp.where(loo == lo, 1.0, 0.0).astype(bf16)
        acc[...] += lax.dot_general(left, right, NT_DIMS, preferred_element_type=f32)

    inv = acc[:half].astype(jnp.int32) * LANES + acc[half:].astype(jnp.int32)
    inv_ref[:half, :] = inv[:, :LANES]
    inv_ref[half:, :] = inv[:, LANES:]


def fetch_kernel(
    req_ref, params_ref, idx_ref,
    out_ref, asked_ref, inv_ref,
    asked_v, asked_s, table, stage, outgoing, acc, send1, recv1, send2, recv2, local,
):
    peers = out_ref.shape[0]
    me = position()
    greet(peers)
    project(params_ref, table, stage)
    hear(peers)

    @pl.loop(1, peers)
    def _(off):
        peer = lax.rem(me + off, peers)
        send(req_ref.at[peer], asked_v.at[me], send1, recv1, peer).start()

    asked_v[me] = req_ref[me]
    await_all(req_ref, asked_v, send1, recv1, peers)
    copy = pltpu.make_async_copy(asked_v, asked_s, local)
    copy.start()
    copy.wait()

    @pl.loop(1, peers)
    def _(off):
        peer = lax.rem(me + off, peers)
        outgoing[peer] = table[asked_s[peer, 0, 0]]
        send(outgoing.at[peer], out_ref.at[me], send2, recv2, peer).start()

    out_ref[me] = table[asked_s[me, 0, 0]]

    @pl.loop(0, peers)
    def _(d):
        asked_ref[d] = asked_s[d, 0, 0]

    invert(idx_ref, inv_ref, acc)
    await_all(outgoing, out_ref, send2, recv2, peers)


def return_kernel(
    grad_ref, inv_ref, out_ref, table, folded, outgoing, send_sem, recv_sem
):
    peers = out_ref.shape[0]
    me = position()
    steps = peers // 8
    greet(peers)
    fill_table(lambda c: grad_ref[c * LANES : (c + 1) * LANES, :], table, EXACT_BACK)
    hear(peers)

    @pl.loop(1, steps + 1)
    def _(n):
        t = lax.rem(me // 8 + n, steps)
        rows = pick(
            inv_ref[rows8(t), :], table, EXACT_BACK, folded,
            lambda c, h: grad_ref[c * LANES + h : c * LANES + h + 1, :],
        )
        for c in range(NFEAT):
            outgoing[pl.ds(t * 8, 8), c, :] = rows[c]

        @pl.when(n < steps)
        def _():
            for q in range(8):
                peer = t * 8 + q
                send(outgoing.at[peer], out_ref.at[me], send_sem, recv_sem, peer).start()

    @pl.loop(0, 8)
    def _(q):
        peer = me // 8 * 8 + q

        @pl.when(peer != me)
        def _():
            send(outgoing.at[peer], out_ref.at[me], send_sem, recv_sem, peer).start()

    out_ref[me] = outgoing[me]
    await_all(outgoing, out_ref, send_sem, recv_sem, peers)


def unproject_kernel(params_ref, asked_ref, grad_ref, out_ref, stage):
    blocks = grad_ref.shape[0]
    stage_blocks(params_ref, asked_ref, stage, blocks)

    @pl.loop(0, blocks // 8)
    def _(i):
        par = [stage[pl.ds(i * 128 + c, 8, stride=16), :] for c in range(NPAR)]
        rows = pl.ds(pl.multiple_of(i * 8, 8), 8)
        grad = [grad_ref[rows, c, :] for c in range(NFEAT)]
        _, pull = jax.vjp(geometry, par[:10])
        res = list(pull(tuple(grad[:5]))[0])
        decay = jnp.exp(-par[10])
        res.append(grad[5] * (decay / (1.0 + decay)))
        res += grad[6:9]
        for c in range(NPAR):
            stage[pl.ds(i * 128 + c, 8, stride=16), :] = res[c]

    @pl.loop(0, blocks, unroll=8)
    def _(r):
        col = pl.multiple_of(asked_ref[r] * LANES, LANES)
        out_ref[:, pl.ds(col, LANES)] = stage[pl.ds(pl.multiple_of(r * 16, 16), NPAR), :]


def split(x, parts):
    out = []
    for _ in range(parts - 1):
        p = x.astype(bf16)
        out.append(p)
        x = x - p.astype(f32)
    out.append(x.astype(bf16))
    return out


def fill_table(read, table, first):
    half = LANES // 2
    for c in range(first, NFEAT):
        xt = read(c).T
        n = 2 * xt.shape[1]
        rem = jnp.concatenate([xt[:half], xt[half:]], axis=1)
        for s, p in enumerate(split(rem, 2)):
            table[(c - first) * half : (c - first + 1) * half, s * n : (s + 1) * n] = p


def rows8(i):
    return pl.ds(pl.multiple_of(i * 8, 8), 8)


def pick(idx8, table, first, folded, row):
    half = LANES // 2
    idx = jnp.concatenate([idx8[q : q + 1] for q in range(8)], axis=1)
    n = idx.shape[1]
    rows = table.shape[1] // 4
    kio = lax.broadcasted_iota(jnp.int32, (2 * rows, n), 0)
    lio = lax.broadcasted_iota(jnp.int32, (half, n), 0)
    hi = ((idx >> 6) & 1) * rows + (idx >> 7)
    mine = lio == (idx & (half - 1))
    oh = jnp.where(kio == hi, 1.0, 0.0).astype(bf16)
    t2 = jnp.dot(table[...], jnp.concatenate([oh, oh], axis=0), preferred_element_type=f32)
    hi8, lo8 = idx8 >> 7, idx8 & (LANES - 1)
    exact = [jnp.zeros((8, LANES), f32)] * first
    for h in range(rows):
        here = hi8 == h
        for c in range(first):
            val = jnp.take_along_axis(
                jnp.broadcast_to(row(c, h), (8, LANES)), lo8, axis=1, mode="promise_in_bounds"
            )
            exact[c] = jnp.where(here, val, exact[c])
    for c in range(first, NFEAT):
        v = jnp.where(mine, t2[(c - first) * half : (c - first + 1) * half], 0.0)
        part = v[0:8]
        for r in range(8, half, 8):
            part = part + v[r : r + 8]
        for q in range(n // LANES):
            folded[c * 64 + q * 8 : c * 64 + q * 8 + 8, :] = part[:, q * LANES : (q + 1) * LANES]
    out = list(exact)
    for c in range(first, NFEAT):
        total = folded[pl.ds(c * 64, 8, stride=8), :]
        for r in range(1, 8):
            total = total + folded[pl.ds(c * 64 + r, 8, stride=8), :]
        out.append(total)
    return out


EXACT = 3
EXACT_BACK = 3
PART = 1024
KC = 16
NB = 6
YS = [n + 0.5 for n in range(SIDE // 2)]


def swap_blocks(rows, lane):
    blk = lane // SIDE
    out = []
    for g in range(8):
        res = None
        for y in range(8):
            shift = ((y - g) * SIDE) % LANES
            r = pltpu.roll(rows[y], shift, 1) if shift else rows[y]
            res = r if res is None else jnp.where(blk == y, r, res)
        out.append(res)
    return out


def render_kernel(
    feat_ref, idx_ref, len_ref, off_ref, cot_ref, spread_ref, reduce_ref,
    img_ref, gsc_ref,
    table, folded, picked, stack, left, bcast, alpha, weight, trans, image, cots, moms, meta,
):
    steps = idx_ref.shape[0] // 8
    fill_table(lambda c: feat_ref[:, c, :], table, EXACT)
    lane = lax.broadcasted_iota(jnp.int32, (8, LANES), 1)
    slot = lane % TG

    def per_tile(read):
        rows = []
        for g in range(8):
            row = jnp.full((1, LANES), read(g * TG), jnp.int32)
            for t in range(1, TG):
                row = jnp.where(slot[:1] == t, read(g * TG + t), row)
            rows.append(row)
        return jnp.concatenate(rows, axis=0)

    meta[0:8, :] = per_tile(lambda t: len_ref[t])
    meta[8:16, :] = per_tile(lambda t: off_ref[0, t]) * SIDE + SIDE // 2
    meta[16:24, :] = per_tile(lambda t: off_ref[1, t]) * SIDE + SIDE // 2
    stack[...] = jnp.zeros_like(stack)
    trans[...] = jnp.ones_like(trans)
    image[...] = jnp.zeros_like(image)
    for c in range(3):
        for h in range(2):
            rows = [cot_ref[c, g * TG : (g + 1) * TG, h * LANES : (h + 1) * LANES] for g in range(8)]
            for y, val in enumerate(swap_blocks(rows, lane)):
                cots[(c * SIDE + h * 8 + y) * 8 : (c * SIDE + h * 8 + y + 1) * 8, :] = val

    def at_step(c, i):
        return pl.ds(pl.multiple_of(c * LANES + i * 8, 8), 8)

    @pl.loop(0, steps)
    def _(i):
        for c, val in enumerate(
            pick(idx_ref[rows8(i), :], table, EXACT, folded, lambda c, h: feat_ref[h, c : c + 1, :])
        ):
            picked[at_step(c, i), :] = val

    @pl.loop(0, steps)
    def _(i):
        f = [picked[at_step(c, i), :] for c in range(NFEAT)]
        live = (i * KC + lane // TG) < meta[0:8, :]
        u = f[0] - meta[8:16, :].astype(f32)
        v = f[1] - meta[16:24, :].astype(f32)
        a, b, c2 = f[2], f[3], f[4]
        picked[at_step(0, i), :] = u
        picked[at_step(1, i), :] = v
        pu = a * u + b * v
        pv = c2 * v + b * u
        k0 = f[5] - 0.5 * (u * pu + v * pv)
        vals = [
            jnp.where(live, LOG2E * k0, -1e30),
            jnp.where(live, LOG2E * pu, 0.0),
            jnp.where(live, LOG2E * pv, 0.0),
            jnp.where(live, (-0.5 * LOG2E) * a, 0.0),
            jnp.where(live, -LOG2E * b, 0.0),
            jnp.where(live, (-0.5 * LOG2E) * c2, 0.0),
            f[6],
            f[7],
            f[8],
        ]
        for n, val in enumerate(vals):
            for s, p in enumerate(split(val, 3)):
                at = s * 8 + n if n < 8 else 24 + s
                stack[pl.ds(at, 8, stride=32), :] = p.astype(f32)
        left[pl.ds(pl.multiple_of(i * LANES, LANES), LANES), :] = jnp.concatenate(
            [stack[:LANES].T, stack[LANES:].T], axis=1
        ).astype(bf16)

    bcast[...] = jnp.dot(left[...], spread_ref[...], preferred_element_type=f32)

    def forward(i):
        for hb in range(2):
            ys = list(range(4 * hb, 4 * hb + 4))
            spots = [(n, sg) for n in ys for sg in (1, -1)]
            yi = {(n, sg): (8 + n if sg > 0 else 7 - n) for n, sg in spots}
            tr = {p: trans[yi[p] * 8 : yi[p] * 8 + 8, :] for p in spots}
            im = {
                (c, p): image[(c * SIDE + yi[p]) * 8 : (c * SIDE + yi[p]) * 8 + 8, :]
                for p in spots
                for c in range(3)
            }
            for kl in range(KC):
                row = pl.ds(pl.multiple_of(i * (KC * 8) + kl * 8, 8), 8)
                pp, qq, rr, cr, cg, cb = [
                    bcast[row, n * LANES : (n + 1) * LANES] for n in range(NB)
                ]
                for n in ys:
                    even = pp + (YS[n] * YS[n]) * rr
                    odd = YS[n] * qq
                    for sg in (1, -1):
                        p = (n, sg)
                        e = jnp.exp2(even + odd if sg > 0 else even - odd)
                        al = jnp.minimum(e, 0.99)
                        w = al * tr[p]
                        tr[p] = tr[p] - w
                        at = pl.ds(pl.multiple_of((i * KC + kl) * PIX // 2 + yi[p] * 8, 8), 8)
                        alpha[at, :] = al
                        weight[at, :] = w
                        for c, col in enumerate((cr, cg, cb)):
                            im[c, p] = im[c, p] + col * w
            for p in spots:
                trans[yi[p] * 8 : yi[p] * 8 + 8, :] = tr[p]
                for c in range(3):
                    image[(c * SIDE + yi[p]) * 8 : (c * SIDE + yi[p]) * 8 + 8, :] = im[c, p]

    def backward(i):
        behind = {y: trans[y * 8 : y * 8 + 8, :] for y in range(SIDE)}
        for kl in reversed(range(KC)):
            row = pl.ds(pl.multiple_of(i * (KC * 8) + kl * 8, 8), 8)
            cols = [bcast[row, n * LANES : (n + 1) * LANES] for n in range(3, NB)]
            acc = [None] * NB

            def add(n, val):
                acc[n] = val if acc[n] is None else acc[n] + val

            for n in range(SIDE // 2):
                dq = {}
                for sg in (1, -1):
                    y = 8 + n if sg > 0 else 7 - n
                    at = pl.ds(pl.multiple_of((i * KC + kl) * PIX // 2 + y * 8, 8), 8)
                    al, w = alpha[at, :], weight[at, :]
                    ct = [cots[(c * SIDE + y) * 8 : (c * SIDE + y + 1) * 8, :] for c in range(3)]
                    d = cols[0] * ct[0] + cols[1] * ct[1] + cols[2] * ct[2] - behind[y]
                    behind[y] = behind[y] + al * d
                    dq[sg] = jnp.where(al < 0.99, w * d, 0.0)
                    for c in range(3):
                        add(3 + c, w * ct[c])
                both, diff = dq[1] + dq[-1], dq[1] - dq[-1]
                add(0, both)
                add(1, YS[n] * diff)
                add(2, (YS[n] * YS[n]) * both)
            for n in range(NB):
                bcast[row, n * LANES : (n + 1) * LANES] = acc[n]
        for y in range(SIDE):
            trans[y * 8 : y * 8 + 8, :] = behind[y]

    @pl.loop(0, steps)
    def _(i):
        forward(i)

    for c in range(3):
        for h in range(2):
            rows = [
                image[(c * SIDE + h * 8 + y) * 8 : (c * SIDE + h * 8 + y + 1) * 8, :]
                for y in range(8)
            ]
            for g, val in enumerate(swap_blocks(rows, lane)):
                img_ref[c, g * TG : (g + 1) * TG, h * LANES : (h + 1) * LANES] = val

    trans[...] = jnp.zeros_like(trans)

    @pl.loop(0, steps)
    def _(n):
        backward(steps - 1 - n)

    batch = 4
    right = jnp.concatenate([reduce_ref[...]] * 3, axis=0)

    @pl.loop(0, steps // batch)
    def _(k):
        rows = pl.ds(pl.multiple_of(k * batch * LANES, LANES), batch * LANES)
        res = jnp.dot(
            jnp.concatenate(split(bcast[rows, :], 3), axis=1), right, preferred_element_type=f32
        )
        for q in range(batch):
            i = k * batch + q
            moms[q * LANES : (q + 1) * LANES, :] = res[q * LANES : (q + 1) * LANES].T
            m = [moms[pl.ds(q * LANES + n, 8, stride=16), :] for n in range(NFEAT)]
            u, v, a, b, c2 = [picked[at_step(n, i), :] for n in range(5)]
            s0, sx, sy, sxx, sxy, syy = m[:6]
            mx = sx - u * s0
            my = sy - v * s0
            out = [
                a * mx + b * my,
                c2 * my + b * mx,
                -0.5 * (sxx - u * (sx + mx)),
                -(sxy - u * sy - v * mx),
                -0.5 * (syy - v * (sy + my)),
                s0,
            ] + m[6:]
            for c in range(NFEAT):
                gsc_ref[at_step(c, i), :] = out[c]


def constants():
    x = np.arange(SIDE) - (SIDE - 1) / 2.0
    one = np.ones(SIDE)
    spread = np.zeros((8, 32, NB, 8, SIDE), np.float32)
    reduce = np.zeros((NB, 8, SIDE, 8, 16), np.float32)
    for g in range(8):
        for s in range(3):
            for row, q, val in (
                (0, 0, one), (1, 0, x), (3, 0, x * x), (2, 1, one), (4, 1, x), (5, 2, one),
                (6, 3, one), (7, 4, one),
            ):
                spread[g, s * 8 + row, q, g] = val
            spread[g, 24 + s, 5, g] = one
        for q, m, val in (
            (0, 0, one), (0, 1, x), (0, 3, x * x), (1, 2, one), (1, 4, x), (2, 5, one),
            (3, 6, one), (4, 7, one), (5, 8, one),
        ):
            reduce[q, g, :, g, m] = val
    return (
        jnp.asarray(spread.reshape(256, NB * LANES), bf16),
        jnp.asarray(reduce.reshape(NB * LANES, LANES), bf16),
    )


VM = pl.BlockSpec(memory_space=pltpu.VMEM)
SM = pl.BlockSpec(memory_space=pltpu.SMEM)
LIMIT = pltpu.CompilerParams(vmem_limit_bytes=50 * 1024 * 1024)


REMOTE = dict(has_side_effects=True, vmem_limit_bytes=40 * 1024 * 1024)


def fetch(requests, params, idx):
    peers = requests.shape[1]
    wanted = jnp.broadcast_to(requests.reshape(peers, 1, 1), (peers, 1, LANES))
    return pl.pallas_call(
        fetch_kernel,
        out_shape=(
            jax.ShapeDtypeStruct((peers, NFEAT, LANES), f32),
            jax.ShapeDtypeStruct((peers,), jnp.int32),
            jax.ShapeDtypeStruct((peers, LANES), jnp.int32),
        ),
        in_specs=[VM, VM, VM],
        out_specs=(VM, SM, VM),
        scratch_shapes=[
            pltpu.VMEM((peers, 1, LANES), jnp.int32),
            pltpu.SMEM((peers, 1, LANES), jnp.int32),
            pltpu.VMEM((peers, NFEAT, LANES), f32),
            pltpu.VMEM((peers * 16, LANES), f32),
            pltpu.VMEM((peers, NFEAT, LANES), f32),
            pltpu.VMEM((peers, 2 * LANES), f32),
        ]
        + [pltpu.SemaphoreType.DMA] * 5,
        compiler_params=pltpu.CompilerParams(collective_id=0, **REMOTE),
        name="fetch",
    )(wanted, params, idx)


def give_back(grads, inv):
    peers = inv.shape[0]
    return pl.pallas_call(
        return_kernel,
        out_shape=jax.ShapeDtypeStruct((peers, NFEAT, LANES), f32),
        in_specs=[VM, VM],
        out_specs=VM,
        scratch_shapes=[
            pltpu.VMEM(((NFEAT - EXACT_BACK) * LANES // 2, 4 * LANES), bf16),
            pltpu.VMEM((NFEAT * 64, LANES), f32),
            pltpu.VMEM((peers, NFEAT, LANES), f32),
        ]
        + [pltpu.SemaphoreType.DMA] * 2,
        compiler_params=pltpu.CompilerParams(collective_id=1, **REMOTE),
        name="give_back",
    )(grads, inv)


def per_device(params, requests, lists, list_len, offsets, cotangent):
    peers = lax.axis_size(AXES)
    g_dev = params.shape[1]
    tiles, length = lists.shape
    steps = length // KC
    idx = lists.reshape(8, TG, steps, KC).transpose(2, 0, 3, 1).reshape(steps * 8, LANES)
    fetched, asked, inv = fetch(requests, params, idx)
    spread, reduce = constants()
    image, gfeat = pl.pallas_call(
        render_kernel,
        out_shape=(
            jax.ShapeDtypeStruct((3, tiles, PIX), f32),
            jax.ShapeDtypeStruct((NFEAT * LANES, LANES), f32),
        ),
        in_specs=[VM, VM, SM, SM, VM, VM, VM],
        out_specs=(VM, VM),
        scratch_shapes=[
            pltpu.VMEM(((NFEAT - EXACT) * LANES // 2, 4 * peers), bf16),
            pltpu.VMEM((NFEAT * 64, LANES), f32),
            pltpu.VMEM((NFEAT * LANES, LANES), f32),
            pltpu.VMEM((256, LANES), f32),
            pltpu.VMEM((length * 8, 256), bf16),
            pltpu.VMEM((length * 8, NB * LANES), f32),
            pltpu.VMEM((length * SIDE * 8, LANES), f32),
            pltpu.VMEM((length * SIDE * 8, LANES), f32),
            pltpu.VMEM((SIDE * 8, LANES), f32),
            pltpu.VMEM((3 * SIDE * 8, LANES), f32),
            pltpu.VMEM((3 * SIDE * 8, LANES), f32),
            pltpu.VMEM((4 * LANES, LANES), f32),
            pltpu.VMEM((24, LANES), jnp.int32),
        ],
        compiler_params=LIMIT,
        name="render",
    )(
        fetched,
        idx,
        list_len,
        offsets.T,
        cotangent.transpose(1, 0, 2),
        spread,
        reduce,
    )

    landed = give_back(gfeat, inv)
    grads = pl.pallas_call(
        unproject_kernel,
        out_shape=jax.ShapeDtypeStruct((NPAR, g_dev), f32),
        in_specs=[VM, SM, VM],
        out_specs=VM,
        scratch_shapes=[pltpu.VMEM((peers * 16, LANES), f32)],
        compiler_params=pltpu.CompilerParams(vmem_limit_bytes=16 * 1024 * 1024),
        name="unproject",
    )(params, asked, landed)
    return image.transpose(1, 0, 2), grads


def solution(mesh):
    in_specs = (
        P(None, AXES),
        P(AXES, None, None),
        P(AXES, None),
        P(AXES),
        P(AXES, None),
        P(AXES, None, None),
    )
    out_specs = (P(AXES, None, None), P(None, AXES))
    return jax.shard_map(
        per_device, mesh=mesh, in_specs=in_specs, out_specs=out_specs, check_vma=False
    )
```

```python
import functools

import jax
import jax.numpy as jnp
import numpy as np
from jax import lax
from jax.experimental import pallas as pl
from jax.experimental.pallas import tpu as pltpu
from jax.sharding import PartitionSpec as P

SIDE = 16
PIX = SIDE * SIDE
FOCAL = 1100.0
LANES = 128
TG = 8
NFEAT = 9
NPAR = 14
LOG2E = 1.4426950408889634
NT_DIMS = (((1,), (1,)), ((), ()))
bf16 = jnp.bfloat16
f32 = jnp.float32
AXES = ("cx", "cy")


def geometry(params):
    focal = jnp.float32(FOCAL)
    xpos, ypos, depth = params[0], params[1], params[2]
    svar = [jnp.exp(2.0 * params[3 + i]) for i in range(3)]
    qnorm = jnp.sqrt(params[6] ** 2 + params[7] ** 2 + params[8] ** 2 + params[9] ** 2)
    qw, qx, qy, qz = (params[6] / qnorm, params[7] / qnorm, params[8] / qnorm, params[9] / qnorm)
    rot = [
        [1.0 - 2.0 * (qy * qy + qz * qz), 2.0 * (qx * qy - qw * qz), 2.0 * (qx * qz + qw * qy)],
        [2.0 * (qx * qy + qw * qz), 1.0 - 2.0 * (qx * qx + qz * qz), 2.0 * (qy * qz - qw * qx)],
        [2.0 * (qx * qz - qw * qy), 2.0 * (qy * qz + qw * qx), 1.0 - 2.0 * (qx * qx + qy * qy)],
    ]

    def sigma(i, j):
        return (
            rot[i][0] * rot[j][0] * svar[0]
            + rot[i][1] * rot[j][1] * svar[1]
            + rot[i][2] * rot[j][2] * svar[2]
        )

    j_diag = focal / depth
    j_xz = -focal * xpos / (depth * depth)
    j_yz = -focal * ypos / (depth * depth)
    s02, s12, s22 = sigma(0, 2), sigma(1, 2), sigma(2, 2)
    cov_a = j_diag * j_diag * sigma(0, 0) + 2.0 * j_diag * j_xz * s02 + j_xz * j_xz * s22 + 0.3
    cov_b = (
        j_diag * j_diag * sigma(0, 1)
        + j_diag * j_yz * s02
        + j_xz * j_diag * s12
        + j_xz * j_yz * s22
    )
    cov_c = j_diag * j_diag * sigma(1, 1) + 2.0 * j_diag * j_yz * s12 + j_yz * j_yz * s22 + 0.3
    determ = cov_a * cov_c - cov_b * cov_b
    return (
        focal * xpos / depth,
        focal * ypos / depth,
        cov_c / determ,
        -cov_b / determ,
        cov_a / determ,
    )


def stage_blocks(params_ref, asked_ref, stage, blocks):
    @pl.loop(0, blocks, unroll=8)
    def _(r):
        col = pl.multiple_of(asked_ref[r] * LANES, LANES)
        stage[pl.ds(pl.multiple_of(r * 16, 16), NPAR), :] = params_ref[:, pl.ds(col, LANES)]


def project(params_ref, out_ref, stage):
    blocks = out_ref.shape[0]

    @pl.loop(0, blocks, unroll=8)
    def _(r):
        col = pl.multiple_of(r * LANES, LANES)
        stage[pl.ds(pl.multiple_of(r * 16, 16), NPAR), :] = params_ref[:, pl.ds(col, LANES)]

    @pl.loop(0, blocks // 8)
    def _(i):
        par = [stage[pl.ds(i * 128 + c, 8, stride=16), :] for c in range(NPAR)]
        feats = list(geometry(par))
        feats.append(-jnp.log(1.0 + jnp.exp(-par[10])))
        feats += par[11:14]
        for c in range(NFEAT):
            stage[pl.ds(i * 128 + c, 8, stride=16), :] = feats[c]

    @pl.loop(0, blocks, unroll=8)
    def _(r):
        out_ref[r] = stage[pl.ds(pl.multiple_of(r * 16, 16), NFEAT), :]


def position():
    return lax.axis_index("cx") * lax.axis_size("cy") + lax.axis_index("cy")


def wrap(value, size):
    return jnp.where(value >= size, value - size, value)


def around(body):
    nx, ny = lax.axis_size("cx"), lax.axis_size("cy")
    cx, cy = lax.axis_index("cx"), lax.axis_index("cy")

    def line(x, first):
        @pl.loop(first, ny)
        def _(dy):
            y = wrap(cy + dy, ny)
            body(x * ny + y, (x, y))

    line(cx, 1)

    @pl.loop(1, nx)
    def _(dx):
        line(wrap(cx + dx, nx), 0)


def greet():
    barrier = pltpu.get_barrier_semaphore()

    def signal(_, spot):
        pl.semaphore_signal(barrier, inc=1, device_id=spot, device_id_type=pl.DeviceIdType.MESH)

    around(signal)


def hear(peers):
    pl.semaphore_wait(pltpu.get_barrier_semaphore(), peers - 1)


def send(source, target, send_sem, recv_sem, spot):
    return pltpu.make_async_remote_copy(
        src_ref=source,
        dst_ref=target,
        send_sem=send_sem,
        recv_sem=recv_sem,
        device_id=spot,
        device_id_type=pl.DeviceIdType.MESH,
    )


def others(source, target, send_sem, recv_sem, peers):
    part = pl.ds(0, peers - 1)
    spot = (lax.axis_index("cx"), lax.axis_index("cy"))
    return send(source.at[part], target.at[part], send_sem, recv_sem, spot)


def invert(idx_ref, inv_ref, acc):
    steps, part = idx_ref.shape[0] // 8, PART
    owners = inv_ref.shape[0]
    half = owners // 2
    hio = lax.broadcasted_iota(jnp.int32, (half, part), 0)
    loo = lax.broadcasted_iota(jnp.int32, (2 * LANES, part), 0)
    spot = lax.broadcasted_iota(jnp.int32, (1, part), 1)
    acc[...] = jnp.zeros_like(acc)

    @pl.loop(0, steps)
    def _(i):
        idx8 = idx_ref[rows8(i), :]
        idx = jnp.concatenate([idx8[q : q + 1] for q in range(8)], axis=1)
        row = idx // LANES
        mine = hio == row % half
        high = (i * (part // LANES) + spot // LANES).astype(f32)
        low = (spot % LANES).astype(f32)
        left = jnp.concatenate(
            [jnp.where(mine, high, 0.0).astype(bf16), jnp.where(mine, low, 0.0).astype(bf16)], axis=0
        )
        lo = row // half * LANES + idx % LANES
        right = jnp.where(loo == lo, 1.0, 0.0).astype(bf16)
        acc[...] += lax.dot_general(left, right, NT_DIMS, preferred_element_type=f32)

    inv = acc[:half].astype(jnp.int32) * LANES + acc[half:].astype(jnp.int32)
    inv_ref[:half, :] = inv[:, :LANES]
    inv_ref[half:, :] = inv[:, LANES:]


def fetch_kernel(
    req_ref, params_ref, idx_ref,
    out_ref, asked_ref, inv_ref,
    asked_v, asked_s, table, stage, outgoing, acc, send1, recv1, send2, recv2, local,
):
    peers = out_ref.shape[0]
    me = position()
    greet()
    project(params_ref, table, stage)
    hear(peers)

    def ask(peer, spot):
        send(req_ref.at[peer], asked_v.at[me], send1, recv1, spot).start()

    def answer(peer, spot):
        outgoing[peer] = table[asked_s[peer, 0, 0]]
        send(outgoing.at[peer], out_ref.at[me], send2, recv2, spot).start()

    around(ask)
    asked_v[me] = req_ref[me]
    rest = others(req_ref, asked_v, send1, recv1, peers)
    rest.wait_send()
    rest.wait_recv()
    copy = pltpu.make_async_copy(asked_v, asked_s, local)
    copy.start()
    copy.wait()
    around(answer)
    out_ref[me] = table[asked_s[me, 0, 0]]

    @pl.loop(0, peers)
    def _(d):
        asked_ref[d] = asked_s[d, 0, 0]

    invert(idx_ref, inv_ref, acc)
    rest = others(outgoing, out_ref, send2, recv2, peers)
    rest.wait_send()
    rest.wait_recv()


def return_kernel(
    grad_ref, inv_ref, out_ref, table, folded, outgoing, send_sem, recv_sem
):
    peers = out_ref.shape[0]
    me = position()
    steps = peers // 8
    greet()
    fill_table(lambda c: grad_ref[c * LANES : (c + 1) * LANES, :], table, EXACT_BACK)
    minor = lax.axis_size("cy")

    def send_group(t):
        for q in range(8):
            spot = (t * 8 // minor, t * 8 % minor + q)
            send(outgoing.at[t * 8 + q], out_ref.at[me], send_sem, recv_sem, spot).start()

    @pl.loop(1, steps + 1)
    def _(n):
        t = wrap(me // 8 + n, steps)
        rows = pick(
            inv_ref[rows8(t), :], table, EXACT_BACK, folded,
            lambda c, h: grad_ref[c * LANES + h : c * LANES + h + 1, :],
        )
        for c in range(NFEAT):
            outgoing[pl.ds(t * 8, 8), c, :] = rows[c]

        @pl.when(n == HEAR)
        def _():
            hear(peers)

            @pl.loop(1, HEAR)
            def _(k):
                send_group(wrap(me // 8 + k, steps))

        @pl.when((n >= HEAR) & (n < steps))
        def _():
            send_group(t)

        major, first = t * 8 // minor, t * 8 % minor

        @pl.when(n == steps)
        def _():
            for q in range(8):

                @pl.when(t * 8 + q != me)
                def _():
                    send(
                        outgoing.at[t * 8 + q], out_ref.at[me], send_sem, recv_sem,
                        (major, first + q),
                    ).start()

    out_ref[me] = outgoing[me]
    rest = others(outgoing, out_ref, send_sem, recv_sem, peers)
    rest.wait_send()
    rest.wait_recv()


def unproject_kernel(params_ref, asked_ref, grad_ref, out_ref, stage):
    blocks = grad_ref.shape[0]
    stage_blocks(params_ref, asked_ref, stage, blocks)

    @pl.loop(0, blocks // 8, unroll=4)
    def _(i):
        par = [stage[pl.ds(i * 128 + c, 8, stride=16), :] for c in range(NPAR)]
        rows = pl.ds(pl.multiple_of(i * 8, 8), 8)
        grad = [grad_ref[rows, c, :] for c in range(NFEAT)]
        _, pull = jax.vjp(geometry, par[:10])
        res = list(pull(tuple(grad[:5]))[0])
        decay = jnp.exp(-par[10])
        res.append(grad[5] * (decay / (1.0 + decay)))
        res += grad[6:9]
        for c in range(NPAR):
            stage[pl.ds(i * 128 + c, 8, stride=16), :] = res[c]

    @pl.loop(0, blocks, unroll=8)
    def _(r):
        col = pl.multiple_of(asked_ref[r] * LANES, LANES)
        out_ref[:, pl.ds(col, LANES)] = stage[pl.ds(pl.multiple_of(r * 16, 16), NPAR), :]


def split(x, parts):
    out = []
    for _ in range(parts - 1):
        p = x.astype(bf16)
        out.append(p)
        x = x - p.astype(f32)
    out.append(x.astype(bf16))
    return out


def fill_table(read, table, first):
    half = LANES // 2
    for c in range(first, NFEAT):
        xt = read(c).T
        n = 2 * xt.shape[1]
        rem = jnp.concatenate([xt[:half], xt[half:]], axis=1)
        for s, p in enumerate(split(rem, 2)):
            table[(c - first) * half : (c - first + 1) * half, s * n : (s + 1) * n] = p


def rows8(i):
    return pl.ds(pl.multiple_of(i * 8, 8), 8)


def pick(idx8, table, first, folded, row):
    half = LANES // 2
    idx = jnp.concatenate([idx8[q : q + 1] for q in range(8)], axis=1)
    n = idx.shape[1]
    rows = table.shape[1] // 4
    kio = lax.broadcasted_iota(jnp.int32, (2 * rows, n), 0)
    lio = lax.broadcasted_iota(jnp.int32, (half, n), 0)
    hi = ((idx >> 6) & 1) * rows + (idx >> 7)
    mine = lio == (idx & (half - 1))
    oh = jnp.where(kio == hi, 1.0, 0.0).astype(bf16)
    t2 = jnp.dot(table[...], jnp.concatenate([oh, oh], axis=0), preferred_element_type=f32)
    hi8, lo8 = idx8 >> 7, idx8 & (LANES - 1)
    exact = [jnp.zeros((8, LANES), f32)] * first
    for h in range(rows):
        here = hi8 == h
        for c in range(first):
            val = jnp.take_along_axis(
                jnp.broadcast_to(row(c, h), (8, LANES)), lo8, axis=1, mode="promise_in_bounds"
            )
            exact[c] = jnp.where(here, val, exact[c])
    for c in range(first, NFEAT):
        v = jnp.where(mine, t2[(c - first) * half : (c - first + 1) * half], 0.0)
        part = v[0:8]
        for r in range(8, half, 8):
            part = part + v[r : r + 8]
        for q in range(n // LANES):
            folded[c * 64 + q * 8 : c * 64 + q * 8 + 8, :] = part[:, q * LANES : (q + 1) * LANES]
    out = list(exact)
    for c in range(first, NFEAT):
        total = folded[pl.ds(c * 64, 8, stride=8), :]
        for r in range(1, 8):
            total = total + folded[pl.ds(c * 64 + r, 8, stride=8), :]
        out.append(total)
    return out


EXACT = 3
EXACT_BACK = 3
HEAR = 6
PART = 1024
KC = 16
NB = 6
YS = [n + 0.5 for n in range(SIDE // 2)]


def swap_blocks(rows, lane):
    blk = lane // SIDE
    out = []
    for g in range(8):
        res = None
        for y in range(8):
            shift = ((y - g) * SIDE) % LANES
            r = pltpu.roll(rows[y], shift, 1) if shift else rows[y]
            res = r if res is None else jnp.where(blk == y, r, res)
        out.append(res)
    return out


def render_kernel(
    feat_ref, idx_ref, len_ref, off_ref, cot_ref, spread_ref, reduce_ref,
    img_ref, gsc_ref,
    table, folded, picked, stack, left, bcast, alpha, weight, trans, image, cots, sums, moms, meta,
):
    steps = idx_ref.shape[0] // 8
    fill_table(lambda c: feat_ref[:, c, :], table, EXACT)
    lane = lax.broadcasted_iota(jnp.int32, (8, LANES), 1)
    slot = lane % TG

    def per_tile(read):
        rows = []
        for g in range(8):
            row = jnp.full((1, LANES), read(g * TG), jnp.int32)
            for t in range(1, TG):
                row = jnp.where(slot[:1] == t, read(g * TG + t), row)
            rows.append(row)
        return jnp.concatenate(rows, axis=0)

    meta[0:8, :] = per_tile(lambda t: len_ref[t])
    meta[8:16, :] = per_tile(lambda t: off_ref[0, t]) * SIDE + SIDE // 2
    meta[16:24, :] = per_tile(lambda t: off_ref[1, t]) * SIDE + SIDE // 2
    stack[...] = jnp.zeros_like(stack)
    trans[...] = jnp.ones_like(trans)
    image[...] = jnp.zeros_like(image)
    for c in range(3):
        for h in range(2):
            rows = [cot_ref[c, g * TG : (g + 1) * TG, h * LANES : (h + 1) * LANES] for g in range(8)]
            for y, val in enumerate(swap_blocks(rows, lane)):
                cots[(c * SIDE + h * 8 + y) * 8 : (c * SIDE + h * 8 + y + 1) * 8, :] = val

    def at_step(c, i):
        return pl.ds(pl.multiple_of(c * LANES + i * 8, 8), 8)

    @pl.loop(0, steps)
    def _(i):
        for c, val in enumerate(
            pick(idx_ref[rows8(i), :], table, EXACT, folded, lambda c, h: feat_ref[h, c : c + 1, :])
        ):
            picked[at_step(c, i), :] = val

    def coefficients(i, stack):
        f = [picked[at_step(c, i), :] for c in range(NFEAT)]
        live = (i * KC + lane // TG) < meta[0:8, :]
        u = f[0] - meta[8:16, :].astype(f32)
        v = f[1] - meta[16:24, :].astype(f32)
        a, b, c2 = f[2], f[3], f[4]
        picked[at_step(0, i), :] = u
        picked[at_step(1, i), :] = v
        pu = a * u + b * v
        pv = c2 * v + b * u
        k0 = f[5] - 0.5 * (u * pu + v * pv)
        vals = [
            jnp.where(live, LOG2E * k0, -1e30),
            jnp.where(live, LOG2E * pu, 0.0),
            jnp.where(live, LOG2E * pv, 0.0),
            jnp.where(live, (-0.5 * LOG2E) * a, 0.0),
            jnp.where(live, -LOG2E * b, 0.0),
            jnp.where(live, (-0.5 * LOG2E) * c2, 0.0),
            f[6],
            f[7],
            f[8],
        ]
        for n, val in enumerate(vals):
            for s, p in enumerate(split(val, 3)):
                at = s * 8 + n if n < 8 else 24 + s
                stack[pl.ds(at, 8, stride=32), :] = p.astype(f32)
        left[pl.ds(pl.multiple_of(i * LANES, LANES), LANES), :] = jnp.concatenate(
            [stack[:LANES].T, stack[LANES:].T], axis=1
        ).astype(bf16)

    @pl.loop(0, steps // 4)
    def _(j):
        for q in range(4):
            coefficients(j * 4 + q, stack.at[q * 256 : (q + 1) * 256])

    bcast[...] = jnp.dot(left[...], spread_ref[...], preferred_element_type=f32)

    def forward(i):
        for hb in range(2):
            ys = list(range(4 * hb, 4 * hb + 4))
            spots = [(n, sg) for n in ys for sg in (1, -1)]
            yi = {(n, sg): (8 + n if sg > 0 else 7 - n) for n, sg in spots}
            tr = {p: trans[yi[p] * 8 : yi[p] * 8 + 8, :] for p in spots}
            im = {
                (c, p): image[(c * SIDE + yi[p]) * 8 : (c * SIDE + yi[p]) * 8 + 8, :]
                for p in spots
                for c in range(3)
            }
            for kl in range(KC):
                row = pl.ds(pl.multiple_of(i * (KC * 8) + kl * 8, 8), 8)
                pp, qq, rr, cr, cg, cb = [
                    bcast[row, n * LANES : (n + 1) * LANES] for n in range(NB)
                ]
                for n in ys:
                    even = pp + (YS[n] * YS[n]) * rr
                    odd = YS[n] * qq
                    for sg in (1, -1):
                        p = (n, sg)
                        e = jnp.exp2(even + odd if sg > 0 else even - odd)
                        al = jnp.minimum(e, 0.99)
                        w = al * tr[p]
                        tr[p] = tr[p] - w
                        at = pl.ds(pl.multiple_of((i * KC + kl) * PIX // 2 + yi[p] * 8, 8), 8)
                        alpha[at, :] = al
                        weight[at, :] = w
                        for c, col in enumerate((cr, cg, cb)):
                            im[c, p] = im[c, p] + col * w
            for p in spots:
                trans[yi[p] * 8 : yi[p] * 8 + 8, :] = tr[p]
                for c in range(3):
                    image[(c * SIDE + yi[p]) * 8 : (c * SIDE + yi[p]) * 8 + 8, :] = im[c, p]

    def backward(i):
        for hb in range(2):
            ns = range(4 * hb, 4 * hb + 4)
            ys = [y for n in ns for y in (8 + n, 7 - n)]
            behind = {y: trans[y * 8 : y * 8 + 8, :] for y in ys}
            ct = {
                (c, y): cots[(c * SIDE + y) * 8 : (c * SIDE + y + 1) * 8, :]
                for y in ys
                for c in range(3)
            }
            for kl in reversed(range(KC)):
                row = pl.ds(pl.multiple_of(i * (KC * 8) + kl * 8, 8), 8)
                cols = [bcast[row, n * LANES : (n + 1) * LANES] for n in range(3, NB)]
                acc = [None] * NB

                def add(n, val):
                    acc[n] = val if acc[n] is None else acc[n] + val

                for n in ns:
                    dq = {}
                    for sg in (1, -1):
                        y = 8 + n if sg > 0 else 7 - n
                        at = pl.ds(pl.multiple_of((i * KC + kl) * PIX // 2 + y * 8, 8), 8)
                        al, w = alpha[at, :], weight[at, :]
                        d = (
                            cols[0] * ct[0, y] + cols[1] * ct[1, y] + cols[2] * ct[2, y] - behind[y]
                        )
                        behind[y] = behind[y] + al * d
                        dq[sg] = jnp.where(al < 0.99, w * d, 0.0)
                        for c in range(3):
                            add(3 + c, w * ct[c, y])
                    both, diff = dq[1] + dq[-1], dq[1] - dq[-1]
                    add(0, both)
                    add(1, YS[n] * diff)
                    add(2, (YS[n] * YS[n]) * both)
                for n in range(NB):
                    at = n * LANES
                    if hb == 0:
                        sums[kl * 8 : kl * 8 + 8, at : at + LANES] = acc[n]
                    else:
                        bcast[row, at : at + LANES] = (
                            sums[kl * 8 : kl * 8 + 8, at : at + LANES] + acc[n]
                        )
            for y in ys:
                trans[y * 8 : y * 8 + 8, :] = behind[y]

    @pl.loop(0, steps)
    def _(i):
        forward(i)

    for c in range(3):
        for h in range(2):
            rows = [
                image[(c * SIDE + h * 8 + y) * 8 : (c * SIDE + h * 8 + y + 1) * 8, :]
                for y in range(8)
            ]
            for g, val in enumerate(swap_blocks(rows, lane)):
                img_ref[c, g * TG : (g + 1) * TG, h * LANES : (h + 1) * LANES] = val

    trans[...] = jnp.zeros_like(trans)

    @pl.loop(0, steps)
    def _(n):
        backward(steps - 1 - n)

    batch = 4
    right = jnp.concatenate([reduce_ref[...]] * 3, axis=0)

    @pl.loop(0, steps // batch)
    def _(k):
        rows = pl.ds(pl.multiple_of(k * batch * LANES, LANES), batch * LANES)
        res = jnp.dot(
            jnp.concatenate(split(bcast[rows, :], 3), axis=1), right, preferred_element_type=f32
        )
        for q in range(batch):
            i = k * batch + q
            moms[q * LANES : (q + 1) * LANES, :] = res[q * LANES : (q + 1) * LANES].T
            m = [moms[pl.ds(q * LANES + n, 8, stride=16), :] for n in range(NFEAT)]
            u, v, a, b, c2 = [picked[at_step(n, i), :] for n in range(5)]
            s0, sx, sy, sxx, sxy, syy = m[:6]
            mx = sx - u * s0
            my = sy - v * s0
            out = [
                a * mx + b * my,
                c2 * my + b * mx,
                -0.5 * (sxx - u * (sx + mx)),
                -(sxy - u * sy - v * mx),
                -0.5 * (syy - v * (sy + my)),
                s0,
            ] + m[6:]
            for c in range(NFEAT):
                gsc_ref[at_step(c, i), :] = out[c]


def constants():
    x = np.arange(SIDE) - (SIDE - 1) / 2.0
    one = np.ones(SIDE)
    spread = np.zeros((8, 32, NB, 8, SIDE), np.float32)
    reduce = np.zeros((NB, 8, SIDE, 8, 16), np.float32)
    for g in range(8):
        for s in range(3):
            for row, q, val in (
                (0, 0, one), (1, 0, x), (3, 0, x * x), (2, 1, one), (4, 1, x), (5, 2, one),
                (6, 3, one), (7, 4, one),
            ):
                spread[g, s * 8 + row, q, g] = val
            spread[g, 24 + s, 5, g] = one
        for q, m, val in (
            (0, 0, one), (0, 1, x), (0, 3, x * x), (1, 2, one), (1, 4, x), (2, 5, one),
            (3, 6, one), (4, 7, one), (5, 8, one),
        ):
            reduce[q, g, :, g, m] = val
    return (
        jnp.asarray(spread.reshape(256, NB * LANES), bf16),
        jnp.asarray(reduce.reshape(NB * LANES, LANES), bf16),
    )


VM = pl.BlockSpec(memory_space=pltpu.VMEM)
SM = pl.BlockSpec(memory_space=pltpu.SMEM)
LIMIT = pltpu.CompilerParams(vmem_limit_bytes=50 * 1024 * 1024)


REMOTE = dict(has_side_effects=True, vmem_limit_bytes=40 * 1024 * 1024)


def fetch(requests, params, idx):
    peers = requests.shape[1]
    wanted = jnp.broadcast_to(requests.reshape(peers, 1, 1), (peers, 1, LANES))
    return pl.pallas_call(
        fetch_kernel,
        out_shape=(
            jax.ShapeDtypeStruct((peers, NFEAT, LANES), f32),
            jax.ShapeDtypeStruct((peers,), jnp.int32),
            jax.ShapeDtypeStruct((peers, LANES), jnp.int32),
        ),
        in_specs=[VM, VM, VM],
        out_specs=(VM, SM, VM),
        scratch_shapes=[
            pltpu.VMEM((peers, 1, LANES), jnp.int32),
            pltpu.SMEM((peers, 1, LANES), jnp.int32),
            pltpu.VMEM((peers, NFEAT, LANES), f32),
            pltpu.VMEM((peers * 16, LANES), f32),
            pltpu.VMEM((peers, NFEAT, LANES), f32),
            pltpu.VMEM((peers, 2 * LANES), f32),
        ]
        + [pltpu.SemaphoreType.DMA] * 5,
        compiler_params=pltpu.CompilerParams(collective_id=0, **REMOTE),
        name="fetch",
    )(wanted, params, idx)


def give_back(grads, inv):
    peers = inv.shape[0]
    return pl.pallas_call(
        return_kernel,
        out_shape=jax.ShapeDtypeStruct((peers, NFEAT, LANES), f32),
        in_specs=[VM, VM],
        out_specs=VM,
        scratch_shapes=[
            pltpu.VMEM(((NFEAT - EXACT_BACK) * LANES // 2, 4 * LANES), bf16),
            pltpu.VMEM((NFEAT * 64, LANES), f32),
            pltpu.VMEM((peers, NFEAT, LANES), f32),
        ]
        + [pltpu.SemaphoreType.DMA] * 2,
        compiler_params=pltpu.CompilerParams(collective_id=1, **REMOTE),
        name="give_back",
    )(grads, inv)


def per_device(params, requests, lists, list_len, offsets, cotangent):
    peers = lax.axis_size(AXES)
    g_dev = params.shape[1]
    tiles, length = lists.shape
    steps = length // KC
    idx = lists.reshape(8, TG, steps, KC).transpose(2, 0, 3, 1).reshape(steps * 8, LANES)
    fetched, asked, inv = fetch(requests, params, idx)
    spread, reduce = constants()
    image, gfeat = pl.pallas_call(
        render_kernel,
        out_shape=(
            jax.ShapeDtypeStruct((3, tiles, PIX), f32),
            jax.ShapeDtypeStruct((NFEAT * LANES, LANES), f32),
        ),
        in_specs=[VM, VM, SM, SM, VM, VM, VM],
        out_specs=(VM, VM),
        scratch_shapes=[
            pltpu.VMEM(((NFEAT - EXACT) * LANES // 2, 4 * peers), bf16),
            pltpu.VMEM((NFEAT * 64, LANES), f32),
            pltpu.VMEM((NFEAT * LANES, LANES), f32),
            pltpu.VMEM((4 * 256, LANES), f32),
            pltpu.VMEM((length * 8, 256), bf16),
            pltpu.VMEM((length * 8, NB * LANES), f32),
            pltpu.VMEM((length * SIDE * 8, LANES), f32),
            pltpu.VMEM((length * SIDE * 8, LANES), f32),
            pltpu.VMEM((SIDE * 8, LANES), f32),
            pltpu.VMEM((3 * SIDE * 8, LANES), f32),
            pltpu.VMEM((3 * SIDE * 8, LANES), f32),
            pltpu.VMEM((KC * 8, NB * LANES), f32),
            pltpu.VMEM((4 * LANES, LANES), f32),
            pltpu.VMEM((24, LANES), jnp.int32),
        ],
        compiler_params=LIMIT,
        name="render",
    )(
        fetched,
        idx,
        list_len,
        offsets.T,
        cotangent.transpose(1, 0, 2),
        spread,
        reduce,
    )

    landed = give_back(gfeat, inv)
    grads = pl.pallas_call(
        unproject_kernel,
        out_shape=jax.ShapeDtypeStruct((NPAR, g_dev), f32),
        in_specs=[VM, SM, VM],
        out_specs=VM,
        scratch_shapes=[pltpu.VMEM((peers * 16, LANES), f32)],
        compiler_params=pltpu.CompilerParams(vmem_limit_bytes=16 * 1024 * 1024),
        name="unproject",
    )(params, asked, landed)
    return image.transpose(1, 0, 2), grads


def solution(mesh):
    in_specs = (
        P(None, AXES),
        P(AXES, None, None),
        P(AXES, None),
        P(AXES),
        P(AXES, None),
        P(AXES, None, None),
    )
    out_specs = (P(AXES, None, None), P(None, AXES))
    return jax.shard_map(
        per_device, mesh=mesh, in_specs=in_specs, out_specs=out_specs, check_vma=False
    )
```

```python
import functools

import jax
import jax.numpy as jnp
import numpy as np
from jax import lax
from jax.experimental import pallas as pl
from jax.experimental.pallas import tpu as pltpu
from jax.sharding import PartitionSpec as P

SIDE = 16
PIX = SIDE * SIDE
FOCAL = 1100.0
LANES = 128
TG = 8
NFEAT = 9
NPAR = 14
LOG2E = 1.4426950408889634
NT_DIMS = (((1,), (1,)), ((), ()))
bf16 = jnp.bfloat16
f32 = jnp.float32
AXES = ("cx", "cy")


def geometry(params):
    focal = jnp.float32(FOCAL)
    xpos, ypos, depth = params[0], params[1], params[2]
    svar = [jnp.exp(2.0 * params[3 + i]) for i in range(3)]
    qnorm = jnp.sqrt(params[6] ** 2 + params[7] ** 2 + params[8] ** 2 + params[9] ** 2)
    qw, qx, qy, qz = (params[6] / qnorm, params[7] / qnorm, params[8] / qnorm, params[9] / qnorm)
    rot = [
        [1.0 - 2.0 * (qy * qy + qz * qz), 2.0 * (qx * qy - qw * qz), 2.0 * (qx * qz + qw * qy)],
        [2.0 * (qx * qy + qw * qz), 1.0 - 2.0 * (qx * qx + qz * qz), 2.0 * (qy * qz - qw * qx)],
        [2.0 * (qx * qz - qw * qy), 2.0 * (qy * qz + qw * qx), 1.0 - 2.0 * (qx * qx + qy * qy)],
    ]

    def sigma(i, j):
        return (
            rot[i][0] * rot[j][0] * svar[0]
            + rot[i][1] * rot[j][1] * svar[1]
            + rot[i][2] * rot[j][2] * svar[2]
        )

    j_diag = focal / depth
    j_xz = -focal * xpos / (depth * depth)
    j_yz = -focal * ypos / (depth * depth)
    s02, s12, s22 = sigma(0, 2), sigma(1, 2), sigma(2, 2)
    cov_a = j_diag * j_diag * sigma(0, 0) + 2.0 * j_diag * j_xz * s02 + j_xz * j_xz * s22 + 0.3
    cov_b = (
        j_diag * j_diag * sigma(0, 1)
        + j_diag * j_yz * s02
        + j_xz * j_diag * s12
        + j_xz * j_yz * s22
    )
    cov_c = j_diag * j_diag * sigma(1, 1) + 2.0 * j_diag * j_yz * s12 + j_yz * j_yz * s22 + 0.3
    determ = cov_a * cov_c - cov_b * cov_b
    return (
        focal * xpos / depth,
        focal * ypos / depth,
        cov_c / determ,
        -cov_b / determ,
        cov_a / determ,
    )


def stage_blocks(params_ref, asked_ref, stage, blocks):
    @pl.loop(0, blocks, unroll=8)
    def _(r):
        col = pl.multiple_of(asked_ref[0, r] * LANES, LANES)
        stage[pl.ds(pl.multiple_of(r * 16, 16), NPAR), :] = params_ref[:, pl.ds(col, LANES)]


def project(params_ref, out_ref, stage):
    blocks = out_ref.shape[0]

    @pl.loop(0, blocks, unroll=8)
    def _(r):
        col = pl.multiple_of(r * LANES, LANES)
        stage[pl.ds(pl.multiple_of(r * 16, 16), NPAR), :] = params_ref[:, pl.ds(col, LANES)]

    @pl.loop(0, blocks // 8)
    def _(i):
        par = [stage[pl.ds(i * 128 + c, 8, stride=16), :] for c in range(NPAR)]
        feats = list(geometry(par))
        feats.append(-jnp.log(1.0 + jnp.exp(-par[10])))
        feats += par[11:14]
        for c in range(NFEAT):
            stage[pl.ds(i * 128 + c, 8, stride=16), :] = feats[c]

    @pl.loop(0, blocks, unroll=8)
    def _(r):
        out_ref[r] = stage[pl.ds(pl.multiple_of(r * 16, 16), NFEAT), :]


def position():
    return lax.axis_index("cx") * lax.axis_size("cy") + lax.axis_index("cy")


def wrap(value, size):
    return jnp.where(value >= size, value - size, value)


def around(body):
    nx, ny = lax.axis_size("cx"), lax.axis_size("cy")
    cx, cy = lax.axis_index("cx"), lax.axis_index("cy")

    def line(x, first):
        @pl.loop(first, ny)
        def _(dy):
            y = wrap(cy + dy, ny)
            body(x * ny + y, (x, y))

    line(cx, 1)

    @pl.loop(1, nx)
    def _(dx):
        line(wrap(cx + dx, nx), 0)


def greet():
    barrier = pltpu.get_barrier_semaphore()

    def signal(_, spot):
        pl.semaphore_signal(barrier, inc=1, device_id=spot, device_id_type=pl.DeviceIdType.MESH)

    around(signal)


def hear(peers):
    pl.semaphore_wait(pltpu.get_barrier_semaphore(), peers - 1)


def send(source, target, send_sem, recv_sem, spot):
    return pltpu.make_async_remote_copy(
        src_ref=source,
        dst_ref=target,
        send_sem=send_sem,
        recv_sem=recv_sem,
        device_id=spot,
        device_id_type=pl.DeviceIdType.MESH,
    )


def others(source, target, send_sem, recv_sem, peers):
    part = pl.ds(0, peers - 1)
    spot = (lax.axis_index("cx"), lax.axis_index("cy"))
    return send(source.at[part], target.at[part], send_sem, recv_sem, spot)


def invert(idx_ref, inv_ref, acc):
    steps, part = idx_ref.shape[0] // 8, PART
    owners = inv_ref.shape[0]
    half = owners // 2
    hio = lax.broadcasted_iota(jnp.int32, (half, part), 0)
    loo = lax.broadcasted_iota(jnp.int32, (2 * LANES, part), 0)
    spot = lax.broadcasted_iota(jnp.int32, (1, part), 1)
    acc[...] = jnp.zeros_like(acc)

    @pl.loop(0, steps)
    def _(i):
        idx8 = idx_ref[rows8(i), :]
        idx = jnp.concatenate([idx8[q : q + 1] for q in range(8)], axis=1)
        row = idx // LANES
        mine = hio == row % half
        high = (i * (part // LANES) + spot // LANES).astype(f32)
        low = (spot % LANES).astype(f32)
        left = jnp.concatenate(
            [jnp.where(mine, high, 0.0).astype(bf16), jnp.where(mine, low, 0.0).astype(bf16)], axis=0
        )
        lo = row // half * LANES + idx % LANES
        right = jnp.where(loo == lo, 1.0, 0.0).astype(bf16)
        acc[...] += lax.dot_general(left, right, NT_DIMS, preferred_element_type=f32)

    inv = acc[:half].astype(jnp.int32) * LANES + acc[half:].astype(jnp.int32)
    inv_ref[:half, :] = inv[:, :LANES]
    inv_ref[half:, :] = inv[:, LANES:]


def fetch_kernel(
    want_ref, params_ref, idx_ref,
    out_ref, asked_ref, inv_ref,
    req_ref, asked_v, asked_row, asked_s, table, stage, outgoing, acc,
    send1, recv1, send2, recv2, local,
):
    peers = out_ref.shape[0]
    me = position()
    greet()
    wanted = jnp.broadcast_to(want_ref[...], (peers, peers)).T
    req_ref[...] = wanted.reshape(peers, 1, peers)
    project(params_ref, table, stage)
    hear(peers)

    def ask(peer, spot):
        send(req_ref.at[peer], asked_v.at[me], send1, recv1, spot).start()

    def answer(peer, spot):
        outgoing[peer] = table[asked_s[0, peer]]
        send(outgoing.at[peer], out_ref.at[me], send2, recv2, spot).start()

    around(ask)
    asked_v[me] = req_ref[me]
    rest = others(req_ref, asked_v, send1, recv1, peers)
    rest.wait_send()
    rest.wait_recv()
    diagonal = lax.broadcasted_iota(jnp.int32, (peers, LANES), 0) == lax.broadcasted_iota(
        jnp.int32, (peers, LANES), 1
    )
    told = jnp.where(diagonal, asked_v[...].reshape(peers, LANES), 0)
    asked_row[...] = jnp.sum(told, axis=0, keepdims=True)
    asked_ref[...] = asked_row[...]
    copy = pltpu.make_async_copy(asked_row, asked_s, local)
    copy.start()
    copy.wait()
    around(answer)
    out_ref[me] = table[asked_s[0, me]]
    invert(idx_ref, inv_ref, acc)
    rest = others(outgoing, out_ref, send2, recv2, peers)
    rest.wait_send()
    rest.wait_recv()


def return_kernel(
    grad_ref, inv_ref, out_ref, table, folded, outgoing, send_sem, recv_sem
):
    peers = out_ref.shape[0]
    me = position()
    steps = peers // 8
    greet()
    fill_table(lambda c: grad_ref[c * LANES : (c + 1) * LANES, :], table, EXACT_BACK)
    minor = lax.axis_size("cy")

    def send_group(t):
        for q in range(8):
            spot = (t * 8 // minor, t * 8 % minor + q)
            send(outgoing.at[t * 8 + q], out_ref.at[me], send_sem, recv_sem, spot).start()

    @pl.loop(1, steps + 1)
    def _(n):
        t = wrap(me // 8 + n, steps)
        rows = pick(
            inv_ref[rows8(t), :], table, EXACT_BACK, folded,
            lambda c, h: grad_ref[c * LANES + h : c * LANES + h + 1, :],
        )
        for c in range(NFEAT):
            outgoing[pl.ds(t * 8, 8), c, :] = rows[c]

        @pl.when(n == HEAR)
        def _():
            hear(peers)

            @pl.loop(1, HEAR)
            def _(k):
                send_group(wrap(me // 8 + k, steps))

        @pl.when((n >= HEAR) & (n < steps))
        def _():
            send_group(t)

        major, first = t * 8 // minor, t * 8 % minor

        @pl.when(n == steps)
        def _():
            for q in range(8):

                @pl.when(t * 8 + q != me)
                def _():
                    send(
                        outgoing.at[t * 8 + q], out_ref.at[me], send_sem, recv_sem,
                        (major, first + q),
                    ).start()

    out_ref[me] = outgoing[me]
    rest = others(outgoing, out_ref, send_sem, recv_sem, peers)
    rest.wait_send()
    rest.wait_recv()


def unproject_kernel(params_ref, asked_ref, grad_ref, out_ref, stage):
    blocks = grad_ref.shape[0]
    stage_blocks(params_ref, asked_ref, stage, blocks)

    @pl.loop(0, blocks // 8, unroll=4)
    def _(i):
        par = [stage[pl.ds(i * 128 + c, 8, stride=16), :] for c in range(NPAR)]
        rows = pl.ds(pl.multiple_of(i * 8, 8), 8)
        grad = [grad_ref[rows, c, :] for c in range(NFEAT)]
        _, pull = jax.vjp(geometry, par[:10])
        res = list(pull(tuple(grad[:5]))[0])
        decay = jnp.exp(-par[10])
        res.append(grad[5] * (decay / (1.0 + decay)))
        res += grad[6:9]
        for c in range(NPAR):
            stage[pl.ds(i * 128 + c, 8, stride=16), :] = res[c]

    @pl.loop(0, blocks, unroll=8)
    def _(r):
        col = pl.multiple_of(asked_ref[0, r] * LANES, LANES)
        out_ref[:, pl.ds(col, LANES)] = stage[pl.ds(pl.multiple_of(r * 16, 16), NPAR), :]


def split(x, parts):
    out = []
    for _ in range(parts - 1):
        p = x.astype(bf16)
        out.append(p)
        x = x - p.astype(f32)
    out.append(x.astype(bf16))
    return out


def fill_table(read, table, first):
    half = LANES // 2
    for c in range(first, NFEAT):
        xt = read(c).T
        n = 2 * xt.shape[1]
        rem = jnp.concatenate([xt[:half], xt[half:]], axis=1)
        for s, p in enumerate(split(rem, 2)):
            table[(c - first) * half : (c - first + 1) * half, s * n : (s + 1) * n] = p


def rows8(i):
    return pl.ds(pl.multiple_of(i * 8, 8), 8)


def pick(idx8, table, first, folded, row):
    half = LANES // 2
    idx = jnp.concatenate([idx8[q : q + 1] for q in range(8)], axis=1)
    n = idx.shape[1]
    rows = table.shape[1] // 4
    kio = lax.broadcasted_iota(jnp.int32, (2 * rows, n), 0)
    lio = lax.broadcasted_iota(jnp.int32, (half, n), 0)
    hi = ((idx >> 6) & 1) * rows + (idx >> 7)
    mine = lio == (idx & (half - 1))
    oh = jnp.where(kio == hi, 1.0, 0.0).astype(bf16)
    t2 = jnp.dot(table[...], jnp.concatenate([oh, oh], axis=0), preferred_element_type=f32)
    hi8, lo8 = idx8 >> 7, idx8 & (LANES - 1)
    exact = [jnp.zeros((8, LANES), f32)] * first
    for h in range(rows):
        here = hi8 == h
        for c in range(first):
            val = jnp.take_along_axis(
                jnp.broadcast_to(row(c, h), (8, LANES)), lo8, axis=1, mode="promise_in_bounds"
            )
            exact[c] = jnp.where(here, val, exact[c])
    for c in range(first, NFEAT):
        v = jnp.where(mine, t2[(c - first) * half : (c - first + 1) * half], 0.0)
        part = v[0:8]
        for r in range(8, half, 8):
            part = part + v[r : r + 8]
        for q in range(n // LANES):
            folded[c * 64 + q * 8 : c * 64 + q * 8 + 8, :] = part[:, q * LANES : (q + 1) * LANES]
    out = list(exact)
    for c in range(first, NFEAT):
        total = folded[pl.ds(c * 64, 8, stride=8), :]
        for r in range(1, 8):
            total = total + folded[pl.ds(c * 64 + r, 8, stride=8), :]
        out.append(total)
    return out


EXACT = 3
EXACT_BACK = 3
HEAR = 6
PART = 1024
KC = 16
NB = 6
YS = [n + 0.5 for n in range(SIDE // 2)]


def swap_blocks(rows, lane):
    blk = lane // SIDE
    out = []
    for g in range(8):
        res = None
        for y in range(8):
            shift = ((y - g) * SIDE) % LANES
            r = pltpu.roll(rows[y], shift, 1) if shift else rows[y]
            res = r if res is None else jnp.where(blk == y, r, res)
        out.append(res)
    return out


def render_kernel(
    feat_ref, idx_ref, len_ref, off_ref, cot_ref, spread_ref, reduce_ref,
    img_ref, gsc_ref,
    table, folded, picked, stack, left, bcast, alpha, weight, trans, image, cots, sums, moms, meta,
):
    steps = idx_ref.shape[0] // 8
    fill_table(lambda c: feat_ref[:, c, :], table, EXACT)
    lane = lax.broadcasted_iota(jnp.int32, (8, LANES), 1)
    slot = lane % TG

    def per_tile(read):
        rows = []
        for g in range(8):
            row = jnp.full((1, LANES), read(g * TG), jnp.int32)
            for t in range(1, TG):
                row = jnp.where(slot[:1] == t, read(g * TG + t), row)
            rows.append(row)
        return jnp.concatenate(rows, axis=0)

    meta[0:8, :] = per_tile(lambda t: len_ref[t])
    meta[8:16, :] = per_tile(lambda t: off_ref[0, t]) * SIDE + SIDE // 2
    meta[16:24, :] = per_tile(lambda t: off_ref[1, t]) * SIDE + SIDE // 2
    stack[...] = jnp.zeros_like(stack)
    trans[...] = jnp.ones_like(trans)
    image[...] = jnp.zeros_like(image)
    for c in range(3):
        for h in range(2):
            rows = [cot_ref[c, g * TG : (g + 1) * TG, h * LANES : (h + 1) * LANES] for g in range(8)]
            for y, val in enumerate(swap_blocks(rows, lane)):
                cots[(c * SIDE + h * 8 + y) * 8 : (c * SIDE + h * 8 + y + 1) * 8, :] = val

    def at_step(c, i):
        return pl.ds(pl.multiple_of(c * LANES + i * 8, 8), 8)

    @pl.loop(0, steps)
    def _(i):
        for c, val in enumerate(
            pick(idx_ref[rows8(i), :], table, EXACT, folded, lambda c, h: feat_ref[h, c : c + 1, :])
        ):
            picked[at_step(c, i), :] = val

    def coefficients(i, stack):
        f = [picked[at_step(c, i), :] for c in range(NFEAT)]
        live = (i * KC + lane // TG) < meta[0:8, :]
        u = f[0] - meta[8:16, :].astype(f32)
        v = f[1] - meta[16:24, :].astype(f32)
        a, b, c2 = f[2], f[3], f[4]
        picked[at_step(0, i), :] = u
        picked[at_step(1, i), :] = v
        pu = a * u + b * v
        pv = c2 * v + b * u
        k0 = f[5] - 0.5 * (u * pu + v * pv)
        vals = [
            jnp.where(live, LOG2E * k0, -1e30),
            jnp.where(live, LOG2E * pu, 0.0),
            jnp.where(live, LOG2E * pv, 0.0),
            jnp.where(live, (-0.5 * LOG2E) * a, 0.0),
            jnp.where(live, -LOG2E * b, 0.0),
            jnp.where(live, (-0.5 * LOG2E) * c2, 0.0),
            f[6],
            f[7],
            f[8],
        ]
        for n, val in enumerate(vals):
            for s, p in enumerate(split(val, 3)):
                at = s * 8 + n if n < 8 else 24 + s
                stack[pl.ds(at, 8, stride=32), :] = p.astype(f32)
        left[pl.ds(pl.multiple_of(i * LANES, LANES), LANES), :] = jnp.concatenate(
            [stack[:LANES].T, stack[LANES:].T], axis=1
        ).astype(bf16)

    @pl.loop(0, steps // 4)
    def _(j):
        for q in range(4):
            coefficients(j * 4 + q, stack.at[q * 256 : (q + 1) * 256])

    bcast[...] = jnp.dot(left[...], spread_ref[...], preferred_element_type=f32)

    def forward(i):
        for hb in range(2):
            ys = list(range(4 * hb, 4 * hb + 4))
            spots = [(n, sg) for n in ys for sg in (1, -1)]
            yi = {(n, sg): (8 + n if sg > 0 else 7 - n) for n, sg in spots}
            tr = {p: trans[yi[p] * 8 : yi[p] * 8 + 8, :] for p in spots}
            im = {
                (c, p): image[(c * SIDE + yi[p]) * 8 : (c * SIDE + yi[p]) * 8 + 8, :]
                for p in spots
                for c in range(3)
            }
            for kl in range(KC):
                row = pl.ds(pl.multiple_of(i * (KC * 8) + kl * 8, 8), 8)
                pp, qq, rr, cr, cg, cb = [
                    bcast[row, n * LANES : (n + 1) * LANES] for n in range(NB)
                ]
                for n in ys:
                    even = pp + (YS[n] * YS[n]) * rr
                    odd = YS[n] * qq
                    for sg in (1, -1):
                        p = (n, sg)
                        e = jnp.exp2(even + odd if sg > 0 else even - odd)
                        al = jnp.minimum(e, 0.99)
                        w = al * tr[p]
                        tr[p] = tr[p] - w
                        at = pl.ds(pl.multiple_of((i * KC + kl) * PIX // 2 + yi[p] * 8, 8), 8)
                        alpha[at, :] = al
                        weight[at, :] = w
                        for c, col in enumerate((cr, cg, cb)):
                            im[c, p] = im[c, p] + col * w
            for p in spots:
                trans[yi[p] * 8 : yi[p] * 8 + 8, :] = tr[p]
                for c in range(3):
                    image[(c * SIDE + yi[p]) * 8 : (c * SIDE + yi[p]) * 8 + 8, :] = im[c, p]

    def backward(i):
        for hb in range(2):
            ns = range(4 * hb, 4 * hb + 4)
            ys = [y for n in ns for y in (8 + n, 7 - n)]
            behind = {y: trans[y * 8 : y * 8 + 8, :] for y in ys}
            ct = {
                (c, y): cots[(c * SIDE + y) * 8 : (c * SIDE + y + 1) * 8, :]
                for y in ys
                for c in range(3)
            }
            for kl in reversed(range(KC)):
                row = pl.ds(pl.multiple_of(i * (KC * 8) + kl * 8, 8), 8)
                cols = [bcast[row, n * LANES : (n + 1) * LANES] for n in range(3, NB)]
                acc = [None] * NB

                def add(n, val):
                    acc[n] = val if acc[n] is None else acc[n] + val

                for n in ns:
                    dq = {}
                    for sg in (1, -1):
                        y = 8 + n if sg > 0 else 7 - n
                        at = pl.ds(pl.multiple_of((i * KC + kl) * PIX // 2 + y * 8, 8), 8)
                        al, w = alpha[at, :], weight[at, :]
                        d = (
                            cols[0] * ct[0, y] + cols[1] * ct[1, y] + cols[2] * ct[2, y] - behind[y]
                        )
                        behind[y] = behind[y] + al * d
                        dq[sg] = jnp.where(al < 0.99, w * d, 0.0)
                        for c in range(3):
                            add(3 + c, w * ct[c, y])
                    both, diff = dq[1] + dq[-1], dq[1] - dq[-1]
                    add(0, both)
                    add(1, YS[n] * diff)
                    add(2, (YS[n] * YS[n]) * both)
                for n in range(NB):
                    at = n * LANES
                    if hb == 0:
                        sums[kl * 8 : kl * 8 + 8, at : at + LANES] = acc[n]
                    else:
                        bcast[row, at : at + LANES] = (
                            sums[kl * 8 : kl * 8 + 8, at : at + LANES] + acc[n]
                        )
            for y in ys:
                trans[y * 8 : y * 8 + 8, :] = behind[y]

    @pl.loop(0, steps)
    def _(i):
        forward(i)

    for c in range(3):
        for h in range(2):
            rows = [
                image[(c * SIDE + h * 8 + y) * 8 : (c * SIDE + h * 8 + y + 1) * 8, :]
                for y in range(8)
            ]
            for g, val in enumerate(swap_blocks(rows, lane)):
                img_ref[c, g * TG : (g + 1) * TG, h * LANES : (h + 1) * LANES] = val

    trans[...] = jnp.zeros_like(trans)

    @pl.loop(0, steps)
    def _(n):
        backward(steps - 1 - n)

    batch = 4
    right = jnp.concatenate([reduce_ref[...]] * 3, axis=0)

    @pl.loop(0, steps // batch)
    def _(k):
        rows = pl.ds(pl.multiple_of(k * batch * LANES, LANES), batch * LANES)
        res = jnp.dot(
            jnp.concatenate(split(bcast[rows, :], 3), axis=1), right, preferred_element_type=f32
        )
        for q in range(batch):
            i = k * batch + q
            moms[q * LANES : (q + 1) * LANES, :] = res[q * LANES : (q + 1) * LANES].T
            m = [moms[pl.ds(q * LANES + n, 8, stride=16), :] for n in range(NFEAT)]
            u, v, a, b, c2 = [picked[at_step(n, i), :] for n in range(5)]
            s0, sx, sy, sxx, sxy, syy = m[:6]
            mx = sx - u * s0
            my = sy - v * s0
            out = [
                a * mx + b * my,
                c2 * my + b * mx,
                -0.5 * (sxx - u * (sx + mx)),
                -(sxy - u * sy - v * mx),
                -0.5 * (syy - v * (sy + my)),
                s0,
            ] + m[6:]
            for c in range(NFEAT):
                gsc_ref[at_step(c, i), :] = out[c]


def constants():
    x = np.arange(SIDE) - (SIDE - 1) / 2.0
    one = np.ones(SIDE)
    spread = np.zeros((8, 32, NB, 8, SIDE), np.float32)
    reduce = np.zeros((NB, 8, SIDE, 8, 16), np.float32)
    for g in range(8):
        for s in range(3):
            for row, q, val in (
                (0, 0, one), (1, 0, x), (3, 0, x * x), (2, 1, one), (4, 1, x), (5, 2, one),
                (6, 3, one), (7, 4, one),
            ):
                spread[g, s * 8 + row, q, g] = val
            spread[g, 24 + s, 5, g] = one
        for q, m, val in (
            (0, 0, one), (0, 1, x), (0, 3, x * x), (1, 2, one), (1, 4, x), (2, 5, one),
            (3, 6, one), (4, 7, one), (5, 8, one),
        ):
            reduce[q, g, :, g, m] = val
    return (
        jnp.asarray(spread.reshape(256, NB * LANES), bf16),
        jnp.asarray(reduce.reshape(NB * LANES, LANES), bf16),
    )


VM = pl.BlockSpec(memory_space=pltpu.VMEM)
SM = pl.BlockSpec(memory_space=pltpu.SMEM)
LIMIT = pltpu.CompilerParams(vmem_limit_bytes=50 * 1024 * 1024)


REMOTE = dict(has_side_effects=True, vmem_limit_bytes=40 * 1024 * 1024)


def fetch(requests, params, idx):
    peers = requests.shape[1]
    return pl.pallas_call(
        fetch_kernel,
        out_shape=(
            jax.ShapeDtypeStruct((peers, NFEAT, LANES), f32),
            jax.ShapeDtypeStruct((1, peers), jnp.int32),
            jax.ShapeDtypeStruct((peers, LANES), jnp.int32),
        ),
        in_specs=[VM, VM, VM],
        out_specs=(VM, VM, VM),
        scratch_shapes=[
            pltpu.VMEM((peers, 1, LANES), jnp.int32),
            pltpu.VMEM((peers, 1, LANES), jnp.int32),
            pltpu.VMEM((1, LANES), jnp.int32),
            pltpu.SMEM((1, LANES), jnp.int32),
            pltpu.VMEM((peers, NFEAT, LANES), f32),
            pltpu.VMEM((peers * 16, LANES), f32),
            pltpu.VMEM((peers, NFEAT, LANES), f32),
            pltpu.VMEM((peers, 2 * LANES), f32),
        ]
        + [pltpu.SemaphoreType.DMA] * 5,
        compiler_params=pltpu.CompilerParams(collective_id=0, **REMOTE),
        name="fetch",
    )(requests.reshape(1, peers), params, idx)


def give_back(grads, inv):
    peers = inv.shape[0]
    return pl.pallas_call(
        return_kernel,
        out_shape=jax.ShapeDtypeStruct((peers, NFEAT, LANES), f32),
        in_specs=[VM, VM],
        out_specs=VM,
        scratch_shapes=[
            pltpu.VMEM(((NFEAT - EXACT_BACK) * LANES // 2, 4 * LANES), bf16),
            pltpu.VMEM((NFEAT * 64, LANES), f32),
            pltpu.VMEM((peers, NFEAT, LANES), f32),
        ]
        + [pltpu.SemaphoreType.DMA] * 2,
        compiler_params=pltpu.CompilerParams(collective_id=1, **REMOTE),
        name="give_back",
    )(grads, inv)


def per_device(params, requests, lists, list_len, offsets, cotangent):
    peers = lax.axis_size(AXES)
    g_dev = params.shape[1]
    tiles, length = lists.shape
    steps = length // KC
    idx = lists.reshape(8, TG, steps, KC).transpose(2, 0, 3, 1).reshape(steps * 8, LANES)
    fetched, asked, inv = fetch(requests, params, idx)
    spread, reduce = constants()
    image, gfeat = pl.pallas_call(
        render_kernel,
        out_shape=(
            jax.ShapeDtypeStruct((3, tiles, PIX), f32),
            jax.ShapeDtypeStruct((NFEAT * LANES, LANES), f32),
        ),
        in_specs=[VM, VM, SM, SM, VM, VM, VM],
        out_specs=(VM, VM),
        scratch_shapes=[
            pltpu.VMEM(((NFEAT - EXACT) * LANES // 2, 4 * peers), bf16),
            pltpu.VMEM((NFEAT * 64, LANES), f32),
            pltpu.VMEM((NFEAT * LANES, LANES), f32),
            pltpu.VMEM((4 * 256, LANES), f32),
            pltpu.VMEM((length * 8, 256), bf16),
            pltpu.VMEM((length * 8, NB * LANES), f32),
            pltpu.VMEM((length * SIDE * 8, LANES), f32),
            pltpu.VMEM((length * SIDE * 8, LANES), f32),
            pltpu.VMEM((SIDE * 8, LANES), f32),
            pltpu.VMEM((3 * SIDE * 8, LANES), f32),
            pltpu.VMEM((3 * SIDE * 8, LANES), f32),
            pltpu.VMEM((KC * 8, NB * LANES), f32),
            pltpu.VMEM((4 * LANES, LANES), f32),
            pltpu.VMEM((24, LANES), jnp.int32),
        ],
        compiler_params=LIMIT,
        name="render",
    )(
        fetched,
        idx,
        list_len,
        offsets.T,
        cotangent.transpose(1, 0, 2),
        spread,
        reduce,
    )

    landed = give_back(gfeat, inv)
    grads = pl.pallas_call(
        unproject_kernel,
        out_shape=jax.ShapeDtypeStruct((NPAR, g_dev), f32),
        in_specs=[VM, SM, VM],
        out_specs=VM,
        scratch_shapes=[pltpu.VMEM((peers * 16, LANES), f32)],
        compiler_params=pltpu.CompilerParams(vmem_limit_bytes=16 * 1024 * 1024),
        name="unproject",
    )(params, asked, landed)
    return image.transpose(1, 0, 2), grads


def solution(mesh):
    in_specs = (
        P(None, AXES),
        P(AXES, None, None),
        P(AXES, None),
        P(AXES),
        P(AXES, None),
        P(AXES, None, None),
    )
    out_specs = (P(AXES, None, None), P(None, AXES))
    return jax.shard_map(
        per_device, mesh=mesh, in_specs=in_specs, out_specs=out_specs, check_vma=False
    )
```

```python
import functools

import jax
import jax.numpy as jnp
import numpy as np
from jax import lax
from jax.experimental import pallas as pl
from jax.experimental.pallas import tpu as pltpu
from jax.sharding import PartitionSpec as P

SIDE = 16
PIX = SIDE * SIDE
FOCAL = 1100.0
LANES = 128
TG = 8
NFEAT = 9
NPAR = 14
LOG2E = 1.4426950408889634
NT_DIMS = (((1,), (1,)), ((), ()))
bf16 = jnp.bfloat16
f32 = jnp.float32
AXES = ("cx", "cy")


def geometry(params):
    focal = jnp.float32(FOCAL)
    xpos, ypos, depth = params[0], params[1], params[2]
    svar = [jnp.exp(2.0 * params[3 + i]) for i in range(3)]
    qnorm = jnp.sqrt(params[6] ** 2 + params[7] ** 2 + params[8] ** 2 + params[9] ** 2)
    qw, qx, qy, qz = (params[6] / qnorm, params[7] / qnorm, params[8] / qnorm, params[9] / qnorm)
    rot = [
        [1.0 - 2.0 * (qy * qy + qz * qz), 2.0 * (qx * qy - qw * qz), 2.0 * (qx * qz + qw * qy)],
        [2.0 * (qx * qy + qw * qz), 1.0 - 2.0 * (qx * qx + qz * qz), 2.0 * (qy * qz - qw * qx)],
        [2.0 * (qx * qz - qw * qy), 2.0 * (qy * qz + qw * qx), 1.0 - 2.0 * (qx * qx + qy * qy)],
    ]

    def sigma(i, j):
        return (
            rot[i][0] * rot[j][0] * svar[0]
            + rot[i][1] * rot[j][1] * svar[1]
            + rot[i][2] * rot[j][2] * svar[2]
        )

    j_diag = focal / depth
    j_xz = -focal * xpos / (depth * depth)
    j_yz = -focal * ypos / (depth * depth)
    s02, s12, s22 = sigma(0, 2), sigma(1, 2), sigma(2, 2)
    cov_a = j_diag * j_diag * sigma(0, 0) + 2.0 * j_diag * j_xz * s02 + j_xz * j_xz * s22 + 0.3
    cov_b = (
        j_diag * j_diag * sigma(0, 1)
        + j_diag * j_yz * s02
        + j_xz * j_diag * s12
        + j_xz * j_yz * s22
    )
    cov_c = j_diag * j_diag * sigma(1, 1) + 2.0 * j_diag * j_yz * s12 + j_yz * j_yz * s22 + 0.3
    determ = cov_a * cov_c - cov_b * cov_b
    return (
        focal * xpos / depth,
        focal * ypos / depth,
        cov_c / determ,
        -cov_b / determ,
        cov_a / determ,
    )


def stage_blocks(params_ref, asked_ref, stage, blocks):
    @pl.loop(0, blocks, unroll=8)
    def _(r):
        col = pl.multiple_of(asked_ref[0, r] * LANES, LANES)
        stage[pl.ds(pl.multiple_of(r * 16, 16), NPAR), :] = params_ref[:, pl.ds(col, LANES)]


def project(params_ref, out_ref, stage):
    blocks = out_ref.shape[0]

    @pl.loop(0, blocks, unroll=8)
    def _(r):
        col = pl.multiple_of(r * LANES, LANES)
        stage[pl.ds(pl.multiple_of(r * 16, 16), NPAR), :] = params_ref[:, pl.ds(col, LANES)]

    @pl.loop(0, blocks // 8)
    def _(i):
        par = [stage[pl.ds(i * 128 + c, 8, stride=16), :] for c in range(NPAR)]
        feats = list(geometry(par))
        feats.append(-jnp.log(1.0 + jnp.exp(-par[10])))
        feats += par[11:14]
        for c in range(NFEAT):
            stage[pl.ds(i * 128 + c, 8, stride=16), :] = feats[c]

    @pl.loop(0, blocks, unroll=8)
    def _(r):
        out_ref[r] = stage[pl.ds(pl.multiple_of(r * 16, 16), NFEAT), :]


def position():
    return lax.axis_index("cx") * lax.axis_size("cy") + lax.axis_index("cy")


def wrap(value, size):
    return jnp.where(value >= size, value - size, value)


def around(body):
    nx, ny = lax.axis_size("cx"), lax.axis_size("cy")
    cx, cy = lax.axis_index("cx"), lax.axis_index("cy")

    def line(x, first):
        @pl.loop(first, ny)
        def _(dy):
            y = wrap(cy + dy, ny)
            body(x * ny + y, (x, y))

    line(cx, 1)

    @pl.loop(1, nx)
    def _(dx):
        line(wrap(cx + dx, nx), 0)


def greet():
    barrier = pltpu.get_barrier_semaphore()

    def signal(_, spot):
        pl.semaphore_signal(barrier, inc=1, device_id=spot, device_id_type=pl.DeviceIdType.MESH)

    around(signal)


def hear(peers):
    pl.semaphore_wait(pltpu.get_barrier_semaphore(), peers - 1)


def send(source, target, send_sem, recv_sem, spot):
    return pltpu.make_async_remote_copy(
        src_ref=source,
        dst_ref=target,
        send_sem=send_sem,
        recv_sem=recv_sem,
        device_id=spot,
        device_id_type=pl.DeviceIdType.MESH,
    )


def others(source, target, send_sem, recv_sem, peers):
    part = pl.ds(0, peers - 1)
    spot = (lax.axis_index("cx"), lax.axis_index("cy"))
    return send(source.at[part], target.at[part], send_sem, recv_sem, spot)


def invert(idx_ref, inv_ref, acc):
    steps, part = idx_ref.shape[0] // 8, PART
    owners = inv_ref.shape[0]
    half = owners // 2
    hio = lax.broadcasted_iota(jnp.int32, (half, part), 0)
    loo = lax.broadcasted_iota(jnp.int32, (2 * LANES, part), 0)
    spot = lax.broadcasted_iota(jnp.int32, (1, part), 1)
    acc[...] = jnp.zeros_like(acc)

    @pl.loop(0, steps)
    def _(i):
        idx8 = idx_ref[rows8(i), :]
        idx = jnp.concatenate([idx8[q : q + 1] for q in range(8)], axis=1)
        row = idx // LANES
        mine = hio == row % half
        high = (i * (part // LANES) + spot // LANES).astype(f32)
        low = (spot % LANES).astype(f32)
        left = jnp.concatenate(
            [jnp.where(mine, high, 0.0).astype(bf16), jnp.where(mine, low, 0.0).astype(bf16)], axis=0
        )
        lo = row // half * LANES + idx % LANES
        right = jnp.where(loo == lo, 1.0, 0.0).astype(bf16)
        acc[...] += lax.dot_general(left, right, NT_DIMS, preferred_element_type=f32)

    inv = acc[:half].astype(jnp.int32) * LANES + acc[half:].astype(jnp.int32)
    inv_ref[:half, :] = inv[:, :LANES]
    inv_ref[half:, :] = inv[:, LANES:]


def tile_rows(len_ref, off_ref, meta):
    slot = lax.broadcasted_iota(jnp.int32, (1, LANES), 1) % TG

    def per_tile(read):
        rows = []
        for g in range(8):
            row = jnp.full((1, LANES), read(g * TG), jnp.int32)
            for t in range(1, TG):
                row = jnp.where(slot == t, read(g * TG + t), row)
            rows.append(row)
        return jnp.concatenate(rows, axis=0)

    meta[0:8, :] = per_tile(lambda t: len_ref[t])
    meta[8:16, :] = per_tile(lambda t: off_ref[0, t]) * SIDE + SIDE // 2
    meta[16:24, :] = per_tile(lambda t: off_ref[1, t]) * SIDE + SIDE // 2


def fetch_kernel(
    want_ref, params_ref, idx_ref, len_ref, off_ref,
    out_ref, asked_ref, inv_ref, meta_ref,
    req_ref, asked_v, asked_row, asked_s, table, stage, outgoing, acc,
    send1, recv1, send2, recv2, local,
):
    peers = out_ref.shape[0]
    me = position()
    greet()
    wanted = jnp.broadcast_to(want_ref[...], (peers, peers)).T
    req_ref[...] = wanted.reshape(peers, 1, peers)
    project(params_ref, table, stage)
    tile_rows(len_ref, off_ref, meta_ref)
    hear(peers)

    def ask(peer, spot):
        send(req_ref.at[peer], asked_v.at[me], send1, recv1, spot).start()

    def answer(peer, spot):
        outgoing[peer] = table[asked_s[0, peer]]
        send(outgoing.at[peer], out_ref.at[me], send2, recv2, spot).start()

    around(ask)
    asked_v[me] = req_ref[me]
    rest = others(req_ref, asked_v, send1, recv1, peers)
    rest.wait_send()
    rest.wait_recv()
    diagonal = lax.broadcasted_iota(jnp.int32, (peers, LANES), 0) == lax.broadcasted_iota(
        jnp.int32, (peers, LANES), 1
    )
    told = jnp.where(diagonal, asked_v[...].reshape(peers, LANES), 0)
    asked_row[...] = jnp.sum(told, axis=0, keepdims=True)
    asked_ref[...] = asked_row[...]
    copy = pltpu.make_async_copy(asked_row, asked_s, local)
    copy.start()
    copy.wait()
    around(answer)
    out_ref[me] = table[asked_s[0, me]]
    invert(idx_ref, inv_ref, acc)
    rest = others(outgoing, out_ref, send2, recv2, peers)
    rest.wait_send()
    rest.wait_recv()


def return_kernel(
    grad_ref, inv_ref, out_ref, table, folded, outgoing, send_sem, recv_sem
):
    peers = out_ref.shape[0]
    me = position()
    steps = peers // 8
    greet()
    fill_table(lambda c: grad_ref[c * LANES : (c + 1) * LANES, :], table, EXACT_BACK)
    minor = lax.axis_size("cy")

    def send_group(t):
        for q in range(8):
            spot = (t * 8 // minor, t * 8 % minor + q)
            send(outgoing.at[t * 8 + q], out_ref.at[me], send_sem, recv_sem, spot).start()

    @pl.loop(1, steps + 1)
    def _(n):
        t = wrap(me // 8 + n, steps)
        rows = pick(
            inv_ref[rows8(t), :], table, EXACT_BACK, folded,
            lambda c, h: grad_ref[c * LANES + h : c * LANES + h + 1, :],
        )
        for c in range(NFEAT):
            outgoing[pl.ds(t * 8, 8), c, :] = rows[c]

        @pl.when(n == HEAR)
        def _():
            hear(peers)

            @pl.loop(1, HEAR)
            def _(k):
                send_group(wrap(me // 8 + k, steps))

        @pl.when((n >= HEAR) & (n < steps))
        def _():
            send_group(t)

        major, first = t * 8 // minor, t * 8 % minor

        @pl.when(n == steps)
        def _():
            for q in range(8):

                @pl.when(t * 8 + q != me)
                def _():
                    send(
                        outgoing.at[t * 8 + q], out_ref.at[me], send_sem, recv_sem,
                        (major, first + q),
                    ).start()

    out_ref[me] = outgoing[me]
    rest = others(outgoing, out_ref, send_sem, recv_sem, peers)
    rest.wait_send()
    rest.wait_recv()


def unproject_kernel(params_ref, asked_ref, grad_ref, out_ref, stage):
    blocks = grad_ref.shape[0]
    stage_blocks(params_ref, asked_ref, stage, blocks)

    @pl.loop(0, blocks // 8, unroll=4)
    def _(i):
        par = [stage[pl.ds(i * 128 + c, 8, stride=16), :] for c in range(NPAR)]
        rows = pl.ds(pl.multiple_of(i * 8, 8), 8)
        grad = [grad_ref[rows, c, :] for c in range(NFEAT)]
        _, pull = jax.vjp(geometry, par[:10])
        res = list(pull(tuple(grad[:5]))[0])
        decay = jnp.exp(-par[10])
        res.append(grad[5] * (decay / (1.0 + decay)))
        res += grad[6:9]
        for c in range(NPAR):
            stage[pl.ds(i * 128 + c, 8, stride=16), :] = res[c]

    @pl.loop(0, blocks, unroll=8)
    def _(r):
        col = pl.multiple_of(asked_ref[0, r] * LANES, LANES)
        out_ref[:, pl.ds(col, LANES)] = stage[pl.ds(pl.multiple_of(r * 16, 16), NPAR), :]


def split(x, parts):
    out = []
    for _ in range(parts - 1):
        p = x.astype(bf16)
        out.append(p)
        x = x - p.astype(f32)
    out.append(x.astype(bf16))
    return out


def fill_table(read, table, first):
    half = LANES // 2
    for c in range(first, NFEAT):
        xt = read(c).T
        n = 2 * xt.shape[1]
        rem = jnp.concatenate([xt[:half], xt[half:]], axis=1)
        for s, p in enumerate(split(rem, 2)):
            table[(c - first) * half : (c - first + 1) * half, s * n : (s + 1) * n] = p


def rows8(i):
    return pl.ds(pl.multiple_of(i * 8, 8), 8)


def pick(idx8, table, first, folded, row):
    half = LANES // 2
    idx = jnp.concatenate([idx8[q : q + 1] for q in range(8)], axis=1)
    n = idx.shape[1]
    rows = table.shape[1] // 4
    kio = lax.broadcasted_iota(jnp.int32, (2 * rows, n), 0)
    lio = lax.broadcasted_iota(jnp.int32, (half, n), 0)
    hi = ((idx >> 6) & 1) * rows + (idx >> 7)
    mine = lio == (idx & (half - 1))
    oh = jnp.where(kio == hi, 1.0, 0.0).astype(bf16)
    t2 = jnp.dot(table[...], jnp.concatenate([oh, oh], axis=0), preferred_element_type=f32)
    hi8, lo8 = idx8 >> 7, idx8 & (LANES - 1)
    exact = [jnp.zeros((8, LANES), f32)] * first
    for h in range(rows):
        here = hi8 == h
        for c in range(first):
            val = jnp.take_along_axis(
                jnp.broadcast_to(row(c, h), (8, LANES)), lo8, axis=1, mode="promise_in_bounds"
            )
            exact[c] = jnp.where(here, val, exact[c])
    for c in range(first, NFEAT):
        v = jnp.where(mine, t2[(c - first) * half : (c - first + 1) * half], 0.0)
        part = v[0:8]
        for r in range(8, half, 8):
            part = part + v[r : r + 8]
        for q in range(n // LANES):
            folded[c * 64 + q * 8 : c * 64 + q * 8 + 8, :] = part[:, q * LANES : (q + 1) * LANES]
    out = list(exact)
    for c in range(first, NFEAT):
        total = folded[pl.ds(c * 64, 8, stride=8), :]
        for r in range(1, 8):
            total = total + folded[pl.ds(c * 64 + r, 8, stride=8), :]
        out.append(total)
    return out


EXACT = 3
EXACT_BACK = 3
HEAR = 6
PART = 1024
KC = 16
NB = 6
YS = [n + 0.5 for n in range(SIDE // 2)]


def swap_blocks(rows, lane):
    blk = lane // SIDE
    out = []
    for g in range(8):
        res = None
        for y in range(8):
            shift = ((y - g) * SIDE) % LANES
            r = pltpu.roll(rows[y], shift, 1) if shift else rows[y]
            res = r if res is None else jnp.where(blk == y, r, res)
        out.append(res)
    return out


def render_kernel(
    feat_ref, idx_ref, meta, cot_ref, spread_ref, reduce_ref,
    img_ref, gsc_ref,
    table, folded, picked, stack, left, bcast, alpha, weight, trans, image, cots, sums, moms,
):
    steps = idx_ref.shape[0] // 8
    fill_table(lambda c: feat_ref[:, c, :], table, EXACT)
    lane = lax.broadcasted_iota(jnp.int32, (8, LANES), 1)
    stack[...] = jnp.zeros_like(stack)
    trans[...] = jnp.ones_like(trans)
    image[...] = jnp.zeros_like(image)
    for c in range(3):
        for h in range(2):
            rows = [cot_ref[c, g * TG : (g + 1) * TG, h * LANES : (h + 1) * LANES] for g in range(8)]
            for y, val in enumerate(swap_blocks(rows, lane)):
                cots[(c * SIDE + h * 8 + y) * 8 : (c * SIDE + h * 8 + y + 1) * 8, :] = val

    def at_step(c, i):
        return pl.ds(pl.multiple_of(c * LANES + i * 8, 8), 8)

    @pl.loop(0, steps)
    def _(i):
        for c, val in enumerate(
            pick(idx_ref[rows8(i), :], table, EXACT, folded, lambda c, h: feat_ref[h, c : c + 1, :])
        ):
            picked[at_step(c, i), :] = val

    def coefficients(i, stack):
        f = [picked[at_step(c, i), :] for c in range(NFEAT)]
        live = (i * KC + lane // TG) < meta[0:8, :]
        u = f[0] - meta[8:16, :].astype(f32)
        v = f[1] - meta[16:24, :].astype(f32)
        a, b, c2 = f[2], f[3], f[4]
        picked[at_step(0, i), :] = u
        picked[at_step(1, i), :] = v
        pu = a * u + b * v
        pv = c2 * v + b * u
        k0 = f[5] - 0.5 * (u * pu + v * pv)
        vals = [
            jnp.where(live, LOG2E * k0, -1e30),
            jnp.where(live, LOG2E * pu, 0.0),
            jnp.where(live, LOG2E * pv, 0.0),
            jnp.where(live, (-0.5 * LOG2E) * a, 0.0),
            jnp.where(live, -LOG2E * b, 0.0),
            jnp.where(live, (-0.5 * LOG2E) * c2, 0.0),
            f[6],
            f[7],
            f[8],
        ]
        for n, val in enumerate(vals):
            for s, p in enumerate(split(val, 3)):
                at = s * 8 + n if n < 8 else 24 + s
                stack[pl.ds(at, 8, stride=32), :] = p.astype(f32)
        left[pl.ds(pl.multiple_of(i * LANES, LANES), LANES), :] = jnp.concatenate(
            [stack[:LANES].T, stack[LANES:].T], axis=1
        ).astype(bf16)

    @pl.loop(0, steps // 4)
    def _(j):
        for q in range(4):
            coefficients(j * 4 + q, stack.at[q * 256 : (q + 1) * 256])

    bcast[...] = jnp.dot(left[...], spread_ref[...], preferred_element_type=f32)

    def forward(i):
        for hb in range(2):
            ys = list(range(4 * hb, 4 * hb + 4))
            spots = [(n, sg) for n in ys for sg in (1, -1)]
            yi = {(n, sg): (8 + n if sg > 0 else 7 - n) for n, sg in spots}
            tr = {p: trans[yi[p] * 8 : yi[p] * 8 + 8, :] for p in spots}
            im = {
                (c, p): image[(c * SIDE + yi[p]) * 8 : (c * SIDE + yi[p]) * 8 + 8, :]
                for p in spots
                for c in range(3)
            }
            for kl in range(KC):
                row = pl.ds(pl.multiple_of(i * (KC * 8) + kl * 8, 8), 8)
                pp, qq, rr, cr, cg, cb = [
                    bcast[row, n * LANES : (n + 1) * LANES] for n in range(NB)
                ]
                for n in ys:
                    even = pp + (YS[n] * YS[n]) * rr
                    odd = YS[n] * qq
                    for sg in (1, -1):
                        p = (n, sg)
                        e = jnp.exp2(even + odd if sg > 0 else even - odd)
                        al = jnp.minimum(e, 0.99)
                        w = al * tr[p]
                        tr[p] = tr[p] - w
                        at = pl.ds(pl.multiple_of((i * KC + kl) * PIX // 2 + yi[p] * 8, 8), 8)
                        alpha[at, :] = al
                        weight[at, :] = w
                        for c, col in enumerate((cr, cg, cb)):
                            im[c, p] = im[c, p] + col * w
            for p in spots:
                trans[yi[p] * 8 : yi[p] * 8 + 8, :] = tr[p]
                for c in range(3):
                    image[(c * SIDE + yi[p]) * 8 : (c * SIDE + yi[p]) * 8 + 8, :] = im[c, p]

    def backward(i):
        for hb in range(2):
            ns = range(4 * hb, 4 * hb + 4)
            ys = [y for n in ns for y in (8 + n, 7 - n)]
            behind = {y: trans[y * 8 : y * 8 + 8, :] for y in ys}
            ct = {
                (c, y): cots[(c * SIDE + y) * 8 : (c * SIDE + y + 1) * 8, :]
                for y in ys
                for c in range(3)
            }
            for kl in reversed(range(KC)):
                row = pl.ds(pl.multiple_of(i * (KC * 8) + kl * 8, 8), 8)
                cols = [bcast[row, n * LANES : (n + 1) * LANES] for n in range(3, NB)]
                acc = [None] * NB

                def add(n, val):
                    acc[n] = val if acc[n] is None else acc[n] + val

                for n in ns:
                    dq = {}
                    for sg in (1, -1):
                        y = 8 + n if sg > 0 else 7 - n
                        at = pl.ds(pl.multiple_of((i * KC + kl) * PIX // 2 + y * 8, 8), 8)
                        al, w = alpha[at, :], weight[at, :]
                        d = (
                            cols[0] * ct[0, y] + cols[1] * ct[1, y] + cols[2] * ct[2, y] - behind[y]
                        )
                        behind[y] = behind[y] + al * d
                        dq[sg] = jnp.where(al < 0.99, w * d, 0.0)
                        for c in range(3):
                            add(3 + c, w * ct[c, y])
                    both, diff = dq[1] + dq[-1], dq[1] - dq[-1]
                    add(0, both)
                    add(1, YS[n] * diff)
                    add(2, (YS[n] * YS[n]) * both)
                for n in range(NB):
                    at = n * LANES
                    if hb == 0:
                        sums[kl * 8 : kl * 8 + 8, at : at + LANES] = acc[n]
                    else:
                        bcast[row, at : at + LANES] = (
                            sums[kl * 8 : kl * 8 + 8, at : at + LANES] + acc[n]
                        )
            for y in ys:
                trans[y * 8 : y * 8 + 8, :] = behind[y]

    @pl.loop(0, steps)
    def _(i):
        forward(i)

    for c in range(3):
        for h in range(2):
            rows = [
                image[(c * SIDE + h * 8 + y) * 8 : (c * SIDE + h * 8 + y + 1) * 8, :]
                for y in range(8)
            ]
            for g, val in enumerate(swap_blocks(rows, lane)):
                img_ref[c, g * TG : (g + 1) * TG, h * LANES : (h + 1) * LANES] = val

    trans[...] = jnp.zeros_like(trans)

    @pl.loop(0, steps)
    def _(n):
        backward(steps - 1 - n)

    batch = 4
    right = jnp.concatenate([reduce_ref[...]] * 3, axis=0)

    @pl.loop(0, steps // batch)
    def _(k):
        rows = pl.ds(pl.multiple_of(k * batch * LANES, LANES), batch * LANES)
        res = jnp.dot(
            jnp.concatenate(split(bcast[rows, :], 3), axis=1), right, preferred_element_type=f32
        )
        for q in range(batch):
            i = k * batch + q
            moms[q * LANES : (q + 1) * LANES, :] = res[q * LANES : (q + 1) * LANES].T
            m = [moms[pl.ds(q * LANES + n, 8, stride=16), :] for n in range(NFEAT)]
            u, v, a, b, c2 = [picked[at_step(n, i), :] for n in range(5)]
            s0, sx, sy, sxx, sxy, syy = m[:6]
            mx = sx - u * s0
            my = sy - v * s0
            out = [
                a * mx + b * my,
                c2 * my + b * mx,
                -0.5 * (sxx - u * (sx + mx)),
                -(sxy - u * sy - v * mx),
                -0.5 * (syy - v * (sy + my)),
                s0,
            ] + m[6:]
            for c in range(NFEAT):
                gsc_ref[at_step(c, i), :] = out[c]


def constants():
    x = np.arange(SIDE) - (SIDE - 1) / 2.0
    one = np.ones(SIDE)
    spread = np.zeros((8, 32, NB, 8, SIDE), np.float32)
    reduce = np.zeros((NB, 8, SIDE, 8, 16), np.float32)
    for g in range(8):
        for s in range(3):
            for row, q, val in (
                (0, 0, one), (1, 0, x), (3, 0, x * x), (2, 1, one), (4, 1, x), (5, 2, one),
                (6, 3, one), (7, 4, one),
            ):
                spread[g, s * 8 + row, q, g] = val
            spread[g, 24 + s, 5, g] = one
        for q, m, val in (
            (0, 0, one), (0, 1, x), (0, 3, x * x), (1, 2, one), (1, 4, x), (2, 5, one),
            (3, 6, one), (4, 7, one), (5, 8, one),
        ):
            reduce[q, g, :, g, m] = val
    return (
        jnp.asarray(spread.reshape(256, NB * LANES), bf16),
        jnp.asarray(reduce.reshape(NB * LANES, LANES), bf16),
    )


VM = pl.BlockSpec(memory_space=pltpu.VMEM)
SM = pl.BlockSpec(memory_space=pltpu.SMEM)
LIMIT = pltpu.CompilerParams(vmem_limit_bytes=50 * 1024 * 1024)


REMOTE = dict(has_side_effects=True, vmem_limit_bytes=40 * 1024 * 1024)


def fetch(requests, params, idx, lengths, offsets):
    peers = requests.shape[1]
    return pl.pallas_call(
        fetch_kernel,
        out_shape=(
            jax.ShapeDtypeStruct((peers, NFEAT, LANES), f32),
            jax.ShapeDtypeStruct((1, peers), jnp.int32),
            jax.ShapeDtypeStruct((peers, LANES), jnp.int32),
            jax.ShapeDtypeStruct((24, LANES), jnp.int32),
        ),
        in_specs=[VM, VM, VM, SM, SM],
        out_specs=(VM,) * 4,
        scratch_shapes=[
            pltpu.VMEM((peers, 1, LANES), jnp.int32),
            pltpu.VMEM((peers, 1, LANES), jnp.int32),
            pltpu.VMEM((1, LANES), jnp.int32),
            pltpu.SMEM((1, LANES), jnp.int32),
            pltpu.VMEM((peers, NFEAT, LANES), f32),
            pltpu.VMEM((peers * 16, LANES), f32),
            pltpu.VMEM((peers, NFEAT, LANES), f32),
            pltpu.VMEM((peers, 2 * LANES), f32),
        ]
        + [pltpu.SemaphoreType.DMA] * 5,
        compiler_params=pltpu.CompilerParams(collective_id=0, **REMOTE),
        name="fetch",
    )(requests.reshape(1, peers), params, idx, lengths, offsets)


def give_back(grads, inv):
    peers = inv.shape[0]
    return pl.pallas_call(
        return_kernel,
        out_shape=jax.ShapeDtypeStruct((peers, NFEAT, LANES), f32),
        in_specs=[VM, VM],
        out_specs=VM,
        scratch_shapes=[
            pltpu.VMEM(((NFEAT - EXACT_BACK) * LANES // 2, 4 * LANES), bf16),
            pltpu.VMEM((NFEAT * 64, LANES), f32),
            pltpu.VMEM((peers, NFEAT, LANES), f32),
        ]
        + [pltpu.SemaphoreType.DMA] * 2,
        compiler_params=pltpu.CompilerParams(collective_id=1, **REMOTE),
        name="give_back",
    )(grads, inv)


def per_device(params, requests, lists, list_len, offsets, cotangent):
    peers = lax.axis_size(AXES)
    g_dev = params.shape[1]
    tiles, length = lists.shape
    steps = length // KC
    idx = lists.reshape(8, TG, steps, KC).transpose(2, 0, 3, 1).reshape(steps * 8, LANES)
    fetched, asked, inv, meta = fetch(requests, params, idx, list_len, offsets.T)
    spread, reduce = constants()
    image, gfeat = pl.pallas_call(
        render_kernel,
        out_shape=(
            jax.ShapeDtypeStruct((3, tiles, PIX), f32),
            jax.ShapeDtypeStruct((NFEAT * LANES, LANES), f32),
        ),
        in_specs=[VM] * 6,
        out_specs=(VM, VM),
        scratch_shapes=[
            pltpu.VMEM(((NFEAT - EXACT) * LANES // 2, 4 * peers), bf16),
            pltpu.VMEM((NFEAT * 64, LANES), f32),
            pltpu.VMEM((NFEAT * LANES, LANES), f32),
            pltpu.VMEM((4 * 256, LANES), f32),
            pltpu.VMEM((length * 8, 256), bf16),
            pltpu.VMEM((length * 8, NB * LANES), f32),
            pltpu.VMEM((length * SIDE * 8, LANES), f32),
            pltpu.VMEM((length * SIDE * 8, LANES), f32),
            pltpu.VMEM((SIDE * 8, LANES), f32),
            pltpu.VMEM((3 * SIDE * 8, LANES), f32),
            pltpu.VMEM((3 * SIDE * 8, LANES), f32),
            pltpu.VMEM((KC * 8, NB * LANES), f32),
            pltpu.VMEM((4 * LANES, LANES), f32),
        ],
        compiler_params=LIMIT,
        name="render",
    )(
        fetched,
        idx,
        meta,
        cotangent.transpose(1, 0, 2),
        spread,
        reduce,
    )

    landed = give_back(gfeat, inv)
    grads = pl.pallas_call(
        unproject_kernel,
        out_shape=jax.ShapeDtypeStruct((NPAR, g_dev), f32),
        in_specs=[VM, SM, VM],
        out_specs=VM,
        scratch_shapes=[pltpu.VMEM((peers * 16, LANES), f32)],
        compiler_params=pltpu.CompilerParams(vmem_limit_bytes=16 * 1024 * 1024),
        name="unproject",
    )(params, asked, landed)
    return image.transpose(1, 0, 2), grads


def solution(mesh):
    in_specs = (
        P(None, AXES),
        P(AXES, None, None),
        P(AXES, None),
        P(AXES),
        P(AXES, None),
        P(AXES, None, None),
    )
    out_specs = (P(AXES, None, None), P(None, AXES))
    return jax.shard_map(
        per_device, mesh=mesh, in_specs=in_specs, out_specs=out_specs, check_vma=False
    )
```
